256 devices in a mesh: gx: 32 (over x, z), gy: 8 (over y, core).
Axes of the slice: x: 4, y: 4, z: 8, core: 2. Of those that a mesh axis runs over, the one named last changes fastest.
Arguments:
- positions: float32 [3, 2097152], P(None, ('gx', 'gy')), as said below
- velocities: float32 [3, 2097152], P(None, ('gx', 'gy')), may hold values from -3 to 3
- angular_velocity: float32 [3, 2097152], P(None, ('gx', 'gy')), may hold values from -6 to 6
- radius: float32 [2097152], P(('gx', 'gy')), may hold values from 0.3 to 0.5
- cell_index: int32 [2097152], P(('gx', 'gy')), may hold values from 0 to 2047, as said below
- pair_index: int32 [16384, 2, 128], P(('gx', 'gy')), may hold values from 0 to 10239, as said below
- live_blocks: int32 [256], P(('gx', 'gy')), may hold values from 8 to 32, as said below
- fluid_velocity: float32 [3, 64, 64, 128], P(None, 'gx', 'gy')
Outputs:
- particle_force: float32 [3, 2097152], P(None, ('gx', 'gy'))
- particle_torque: float32 [3, 2097152], P(None, ('gx', 'gy'))
- pressure: float32 [64, 64, 128], P('gx', 'gy')
The draws below stay inside these ranges and needn't reach their ends.
Inputs may be any that keep to these rules, and one draw needn't show every extreme that they name: `cell_index`: the cell lies in the device's block; the first 2048 particles of every device lie in the block's last layer along the first dimension. `positions`: each particle lies inside the unit cube of its cell (cells are unit cubes, the grid starts at 0). `pair_index`: A first entry names a particle of the device. A second entry names another particle of the device in the same cell, or, at 8192 + k, particle k of the device one lower along gx with the same gy index, in the cell beside the first particle's along the first dimension; devices at gx index 0 name no such particle. Entries of blocks that are not live are valid too. `live_blocks`: some device has exactly 32 blocks live.
All inputs are finite; a program needn't handle non-finite values.
Results may differ from the reference program's by a relative error of at most 0.0003.
Values sent between devices are 32-bit elements; how exact they have to be, the bound alone decides.
No kernel may reach another device: no remote copies, remote signals or barrier semaphores. Data moves between devices by JAX's collectives and lax.ppermute only.
A program may use at most 128 MiB of HBM per device.

```python
import math
import jax
import jax.numpy as jnp
from jax import lax

CX = 2
CY = 8
CZ = 128
ITERS = 3
P_DEV = 8192
B_DEV = 2048
NB = 64
NPART = 2097152
NX = 64
NY = 64
NZ = 128
N_GX = 32
N_GY = 8


def particle_order(key):
    devices_total = N_GX * N_GY
    key = jax.random.fold_in(key, 101)
    key_low, key_mid, key_rest = jax.random.split(key, 3)
    low_part = jax.vmap(lambda each: jax.random.permutation(each, B_DEV))(jax.random.split(key_low, devices_total))
    mid_part = jax.vmap(lambda each: jax.random.permutation(each, B_DEV))(jax.random.split(key_mid, devices_total))
    pieces = [low_part.astype(jnp.int32), (mid_part + B_DEV).astype(jnp.int32)]
    if P_DEV > 2 * B_DEV:
        rest_part = jax.vmap(lambda each: jax.random.permutation(each, P_DEV - 2 * B_DEV))(jax.random.split(key_rest, devices_total))
        pieces.append((rest_part + 2 * B_DEV).astype(jnp.int32))
    return jnp.concatenate(pieces, 1)


def base_cells(key):
    devices_total = N_GX * N_GY
    groups = P_DEV // 4
    border_groups = B_DEV // 4
    key_layer, key_row, key_depth = jax.random.split(key, 3)
    layer = jax.random.randint(key_layer, (devices_total, groups), 0, CX)
    row_in = jax.random.randint(key_row, (devices_total, groups), 0, CY)
    depth = jax.random.randint(key_depth, (devices_total, groups), 0, CZ)
    lower_row = jnp.roll(row_in[:, :border_groups], N_GY, axis=0)
    lower_depth = jnp.roll(depth[:, :border_groups], N_GY, axis=0)
    layer = layer.at[:, :border_groups].set(CX - 1).at[:, border_groups:2 * border_groups].set(0)
    row_in = row_in.at[:, border_groups:2 * border_groups].set(lower_row)
    depth = depth.at[:, border_groups:2 * border_groups].set(lower_depth)
    cells = (layer * CY + row_in) * CZ + depth
    return jnp.repeat(cells, 4, axis=1).astype(jnp.int32)


def group_cells(key):
    devices_total = N_GX * N_GY
    cells = base_cells(key)
    slot = particle_order(key)
    device_rows = jnp.arange(devices_total, dtype=jnp.int32)[:, None]
    placed = jnp.zeros_like(cells).at[device_rows, slot].set(cells)
    return placed.reshape(-1).astype(jnp.int32)


def draw_cell_index(key, part):
    return group_cells(key)


def draw_positions(key, part):
    cells = group_cells(key)
    key = jax.random.fold_in(key, 3)
    total = N_GX * N_GY * P_DEV
    device_of = jnp.arange(total, dtype=jnp.int32) // P_DEV
    slab = device_of // N_GY
    column = device_of % N_GY
    corner = jnp.stack([slab * CX + cells // (CY * CZ), column * CY + cells // CZ % CY, cells % CZ]).astype(jnp.float32)
    inside = jax.random.uniform(key, (3, total), jnp.float32)
    return corner + inside


def draw_pair_index(key, part):
    slot = particle_order(key)
    key = jax.random.fold_in(key, 5)
    devices_total = N_GX * N_GY
    slots = NB * 128
    groups = P_DEV // 4
    border_groups = B_DEV // 4
    keys = jax.random.split(key, 6)
    shape = (devices_total, slots)
    group = jax.random.randint(keys[0], shape, 0, groups)
    member = jax.random.randint(keys[1], shape, 0, 4)
    partner = (member + jax.random.randint(keys[2], shape, 1, 4)) % 4
    crossing = jax.random.randint(keys[3], shape, 0, 4) == 0
    crossing = crossing & (jnp.arange(devices_total, dtype=jnp.int32)[:, None] >= N_GY)
    border_group = jax.random.randint(keys[4], shape, 0, border_groups)
    ghost_member = jax.random.randint(keys[5], shape, 0, 4)
    first = jnp.where(crossing, 4 * (border_groups + border_group) + member, 4 * group + member)
    second = jnp.where(crossing, P_DEV + 4 * border_group + ghost_member, 4 * group + partner)
    lower_slot = jnp.roll(slot, N_GY, axis=0)
    first_new = jnp.take_along_axis(slot, first.astype(jnp.int32), axis=1)
    own_index = jnp.minimum(second, P_DEV - 1).astype(jnp.int32)
    ghost_index = jnp.clip(second - P_DEV, 0, B_DEV - 1).astype(jnp.int32)
    second_own = jnp.take_along_axis(slot, own_index, axis=1)
    second_ghost = P_DEV + jnp.take_along_axis(lower_slot, ghost_index, axis=1)
    second_new = jnp.where(second < P_DEV, second_own, second_ghost)
    stacked = jnp.stack([first_new.reshape(devices_total * NB, 128), second_new.reshape(devices_total * NB, 128)], 1)
    return stacked.astype(jnp.int32)


def draw_live_blocks(key, part):
    key = jax.random.fold_in(key, 7)
    devices_total = N_GX * N_GY
    key_count, key_most, key_least = jax.random.split(key, 3)
    counts = jax.random.randint(key_count, (devices_total,), NB // 8, NB // 2 + 1)
    busiest = jax.random.randint(key_most, (), 0, devices_total)
    lightest = (busiest + 1 + jax.random.randint(key_least, (), 0, devices_total - 1)) % devices_total
    counts = counts.at[busiest].set(NB // 2).at[lightest].set(NB // 8)
    return counts.astype(jnp.int32)


def draw_fluid_velocity(key, part):
    key = jax.random.fold_in(key, 9)
    height = (jnp.arange(NX, dtype=jnp.float32) + 0.5) / NX
    base = jax.random.normal(key, (3, NX, NY, NZ), jnp.float32)
    scale = 1.0 + 3.0 * height
    return base * scale[None, :, None, None]


def level_of(rng, dims, cuts, smallest, largest):
    def one(axis_at, shards_of):
        draws = jax.random.uniform(jax.random.fold_in(jax.random.fold_in(rng, 6), axis_at), (shards_of,), jnp.float32, smallest / len(cuts), largest / len(cuts))
        return jnp.repeat(jnp.exp(draws), dims[axis_at] // shards_of).reshape((-1,) + (1,) * (len(dims) - axis_at - 1))

    loudness = one(*cuts[0])
    for cut in cuts[1:]:
        loudness = loudness * one(*cut)
    return loudness


def centred(stream_key, extent, scale, reach, cuts=(), kind=jnp.bfloat16):
    values = scale * jax.random.normal(stream_key, extent, jnp.float32)
    if cuts:
        values = values * level_of(stream_key, extent, cuts, -0.22, 0.18)
    return jnp.clip(values, -reach, reach).astype(kind)


def setup_inputs(seed: int = 0) -> dict:
    arg_keys = jax.random.split(jax.random.key(seed), 9)
    return {
        "positions": draw_positions(jax.random.fold_in(arg_keys[8], 71), 0),
        "velocities": centred(arg_keys[1], (3, NPART), 0.5, 3.0, ((1, 256),), jnp.float32),
        "angular_velocity": centred(arg_keys[2], (3, NPART), 1.0, 6.0, ((1, 256),), jnp.float32),
        "radius": jnp.clip(jnp.exp(math.log(0.5) - 0.5108256 * jax.random.uniform(arg_keys[3], (NPART,), jnp.float32) ** level_of(arg_keys[3], (NPART,), ((0, 256),), -0.2, 0.2)), 0.3, 0.5),
        "cell_index": draw_cell_index(jax.random.fold_in(arg_keys[8], 71), 0),
        "pair_index": draw_pair_index(jax.random.fold_in(arg_keys[8], 71), 0),
        "live_blocks": draw_live_blocks(jax.random.fold_in(arg_keys[8], 71), 0),
        "fluid_velocity": draw_fluid_velocity(jax.random.fold_in(arg_keys[8], 71), 0),
    }


STIFFNESS = 4.0
DAMPING = 1.0
FRICTION = 0.5
SLIP_SCALE = 0.1
DRAG_RATE = 3.0
SPHERE = 4.18879020478639

def cross_product(left, right):
    return jnp.stack([left[1] * right[2] - left[2] * right[1], left[2] * right[0] - left[0] * right[2], left[0] * right[1] - left[1] * right[0]])

def contact_terms(pos_first, pos_second, vel_first, vel_second, spin_first, spin_second, rad_first, rad_second):
    offset = pos_second - pos_first
    distance = jnp.sqrt(lax.optimization_barrier(jnp.sum(offset * offset, axis=0)))
    contact_reach = rad_first + rad_second
    normal = offset / jnp.maximum(distance, 0.25 * contact_reach)
    correlation = jnp.maximum(contact_reach - distance, 0.0)
    root_correlation = jnp.sqrt(correlation)
    lever_arm = rad_first * spin_first + rad_second * spin_second
    slip_velocity = vel_second - vel_first - cross_product(lever_arm, normal)
    normal_speed = lax.optimization_barrier(jnp.sum(slip_velocity * normal, axis=0))
    normal_push = STIFFNESS * correlation * root_correlation - DAMPING * root_correlation * normal_speed
    tangent = slip_velocity - normal_speed * normal
    tangent_size = jnp.sqrt(lax.optimization_barrier(jnp.sum(tangent * tangent, axis=0)) + SLIP_SCALE * SLIP_SCALE)
    friction = FRICTION * jnp.abs(normal_push) * tangent / tangent_size
    pair_force = friction - normal_push * normal
    pair_twist = cross_product(normal, friction)
    return (pair_force, rad_first * pair_twist, rad_second * pair_twist)

def faces_of(padded):
    return [padded[2:, 1:-1, 1:-1], padded[:-2, 1:-1, 1:-1], padded[1:-1, 2:, 1:-1], padded[1:-1, :-2, 1:-1], padded[1:-1, 1:-1, 2:], padded[1:-1, 1:-1, :-2]]

def operate_padded(field, padded_field, porosity, padded_porosity):
    result = jnp.zeros_like(field)
    for near_field, near_porosity in zip(faces_of(padded_field), faces_of(padded_porosity)):
        result = result + 0.5 * (porosity + near_porosity) * (field - near_field)
    return result

def reference(positions, velocities, angular_velocity, radius, cell_index, pair_index, live_blocks, fluid_velocity):
    devices_total = N_GX * N_GY
    block_ids = jnp.arange(NB, dtype=jnp.int32)

    def one_device(carry, device):
        blocks = lax.dynamic_slice_in_dim(pair_index, device * NB, NB, 0)
        first_local = blocks[:, 0, :].reshape(-1)
        second_local = blocks[:, 1, :].reshape(-1)
        keep = jnp.broadcast_to((block_ids < live_blocks[device])[:, None], (NB, 128)).reshape(-1).astype(jnp.float32)
        first = device * P_DEV + first_local
        second = jnp.where(second_local < P_DEV, device * P_DEV + second_local, (device - N_GY) * P_DEV + second_local - P_DEV)
        pair_force, twist_first, twist_second = contact_terms(positions[:, first], positions[:, second], velocities[:, first], velocities[:, second], angular_velocity[:, first], angular_velocity[:, second], radius[first], radius[second])
        carry = carry.at[:, first].add(jnp.concatenate([pair_force * keep, twist_first * keep], 0))
        carry = carry.at[:, second].add(jnp.concatenate([-pair_force * keep, twist_second * keep], 0))
        return (carry, None)
    accumulated = jnp.zeros((6, positions.shape[1]), jnp.float32)
    accumulated, unused = lax.scan(one_device, accumulated, jnp.arange(devices_total, dtype=jnp.int32))
    particle_ids = jnp.arange(positions.shape[1], dtype=jnp.int32)
    device_of = particle_ids // P_DEV
    slab = device_of // N_GY
    column = device_of % N_GY
    layer = cell_index // (CY * CZ)
    row_in = cell_index // CZ % CY
    depth = cell_index % CZ
    flat_cell = ((slab * CX + layer) * NY + column * CY + row_in) * NZ + depth
    fluid_flat = fluid_velocity.reshape(3, -1)
    drag = DRAG_RATE * radius * (fluid_flat[:, flat_cell] - velocities)
    particle_force = accumulated[:3] + drag
    particle_torque = accumulated[3:]
    deposit = jnp.zeros((4, NX * NY * NZ), jnp.float32).at[:, flat_cell].add(jnp.concatenate([-drag, (SPHERE * radius * radius * radius)[None]], 0))
    porosity = (1.0 / (1.0 + deposit[3])).reshape(NX, NY, NZ)
    momentum = deposit[:3].reshape(3, NX, NY, NZ)
    padded_momentum = jnp.pad(momentum, ((0, 0), (1, 1), (1, 1), (1, 1)))
    source = 0.5 * (padded_momentum[0, 2:, 1:-1, 1:-1] - padded_momentum[0, :-2, 1:-1, 1:-1])
    source = source + 0.5 * (padded_momentum[1, 1:-1, 2:, 1:-1] - padded_momentum[1, 1:-1, :-2, 1:-1])
    source = source + 0.5 * (padded_momentum[2, 1:-1, 1:-1, 2:] - padded_momentum[2, 1:-1, 1:-1, :-2])
    padded_porosity = jnp.pad(porosity, 1)
    pressure = jnp.zeros_like(source)
    residual = source
    direction = source
    norm_now = jnp.sum(residual * residual)
    for iteration in range(ITERS):
        image = operate_padded(direction, jnp.pad(direction, 1), porosity, padded_porosity)
        alpha = norm_now / jnp.sum(direction * image)
        pressure = pressure + alpha * direction
        residual = residual - alpha * image
        norm_next = jnp.sum(residual * residual)
        direction = residual + norm_next / norm_now * direction
        norm_now = norm_next
    return (particle_force, particle_torque, pressure)
```

```python
import functools

import jax
import jax.numpy as jnp
from jax import lax
from jax.experimental import pallas as pl
from jax.experimental.pallas import tpu as pltpu
from jax.sharding import PartitionSpec as P

STIFFNESS = 4.0
DAMPING = 1.0
FRICTION = 0.5
SLIP_SCALE = 0.1
DRAG_RATE = 3.0
SPHERE = 4.18879020478639

F32 = jnp.float32
BF16 = jnp.bfloat16
BOTH = ("gx", "gy")
VMEM_SPEC = pl.BlockSpec(memory_space=pltpu.VMEM)
SMEM_SPEC = pl.BlockSpec(memory_space=pltpu.SMEM)
PARAMS = pltpu.CompilerParams(vmem_limit_bytes=24 * 1024 * 1024)


def split(x):
    high = x.astype(BF16)
    return high, (x - high.astype(F32)).astype(BF16)


def one_hot(size, index):
    rows = lax.broadcasted_iota(jnp.int32, (size, index.shape[1]), 0)
    return rows == index


def as_bf16(mask):
    return jnp.where(mask, 1.0, 0.0).astype(BF16)


def lanes(block, rows):
    return jnp.concatenate([block[r : r + 1, :] for r in rows], axis=1)


def dot_nt(left, right):
    return lax.dot_general(left, right, (((1,), (1,)), ((), ())), preferred_element_type=F32)


def deposit_kernel(vel, radius, cell, fluid, fields, drag):
    fluid_high, fluid_low = split(fluid[...])
    fluid_table = jnp.concatenate([fluid_high, fluid_low], axis=1)
    total = jnp.zeros((64, 128), F32)
    for g in range(8):
        cells = lanes(cell[8 * g : 8 * g + 8, :], range(8))
        rad = lanes(radius[8 * g : 8 * g + 8, :], range(8))
        here = pl.ds(1024 * g, 1024)
        hot = as_bf16(one_hot(128, cells & 127))
        mask = one_hot(16, cells >> 7)
        seen = jnp.dot(
            fluid_table, jnp.concatenate([hot, hot], axis=0), preferred_element_type=F32
        )
        values = []
        for d in range(3):
            u = jnp.sum(jnp.where(mask, seen[16 * d : 16 * d + 16], 0.0), axis=0, keepdims=True)
            force = DRAG_RATE * rad * (u - vel[d : d + 1, here])
            drag[d : d + 1, here] = force
            values.append(-force)
        values.append(SPHERE * rad * rad * rad)
        spread = jnp.concatenate([jnp.where(mask, v, 0.0) for v in values], axis=0)
        high, low = split(spread)
        total = total + dot_nt(
            jnp.concatenate([high, low], axis=1), jnp.concatenate([hot, hot], axis=1)
        )
    lane = lax.broadcasted_iota(jnp.int32, (16, 128), 1)
    mz = total[32:48]
    up = jnp.where(lane == 127, 0.0, pltpu.roll(mz, 127, 1))
    down = jnp.where(lane == 0, 0.0, pltpu.roll(mz, 1, 1))
    out = [total[0:16], 1.0 / (1.0 + total[48:64]), total[16:32], 0.5 * (up - down)]
    for f in range(4):
        for layer in range(2):
            fields[f, layer] = out[f][8 * layer : 8 * layer + 8]


def table_kernel(place, pos, vel, spin, radius, cell, table, border):
    def dense(ref, d):
        return jnp.concatenate(
            [ref[d : d + 1, 128 * k : 128 * k + 128] for k in range(64)], axis=0
        )

    cells = cell[...]
    rad = radius[...]
    corner = [
        place[0] * 2 + (cells >> 10),
        place[1] * 8 + ((cells >> 7) & 7),
        cells & 127,
    ]
    fields = [dense(pos, d) - corner[d].astype(F32) for d in range(3)]
    fields += [dense(vel, d) for d in range(3)]
    fields += [rad * dense(spin, d) for d in range(3)]
    fields += [rad]
    for f in range(10):
        high, low = split(fields[f])
        rows = pl.ds(32 * f, 32)
        table[rows, 0:128] = high[0:32]
        table[rows, 128:256] = high[32:64]
        table[rows, 256:384] = low[0:32]
        table[rows, 384:512] = low[32:64]
        border[f] = fields[f][0:16] - 1.0 if f == 0 else fields[f][0:16]


def cross(a, b):
    return [
        a[1] * b[2] - a[2] * b[1],
        a[2] * b[0] - a[0] * b[2],
        a[0] * b[1] - a[1] * b[0],
    ]


def dot3(a, b):
    return a[0] * b[0] + a[1] * b[1] + a[2] * b[2]


def contact_terms(first, second):
    offset = [second[d] - first[d] for d in range(3)]
    distance = jnp.sqrt(dot3(offset, offset))
    reach = first[9] + second[9]
    inverse = 1.0 / jnp.maximum(distance, 0.25 * reach)
    normal = [o * inverse for o in offset]
    correlation = jnp.maximum(reach - distance, 0.0)
    root = jnp.sqrt(correlation)
    lever = [first[6 + d] + second[6 + d] for d in range(3)]
    turn = cross(lever, normal)
    slip = [second[3 + d] - first[3 + d] - turn[d] for d in range(3)]
    speed = dot3(slip, normal)
    push = STIFFNESS * correlation * root - DAMPING * root * speed
    tangent = [slip[d] - speed * normal[d] for d in range(3)]
    size = jnp.sqrt(dot3(tangent, tangent) + SLIP_SCALE * SLIP_SCALE)
    scale = FRICTION * jnp.abs(push) / size
    friction = [scale * t for t in tangent]
    force = [friction[d] - push * normal[d] for d in range(3)]
    twist = cross(normal, friction)
    return force, twist


def contact_kernel(live, pairs, table, ghost, drag, force_out, twist_out, returned, seconds, total):
    span = 512
    seconds[0:320, :] = table[...]
    pieces = [
        jnp.concatenate([ghost[f, 0:8, :], ghost[f, 8:16, :]], axis=1) for f in range(10)
    ]
    high, low = split(jnp.concatenate(pieces, axis=0))
    seconds[320:400, 0:256] = high
    seconds[320:400, 256:512] = low
    total[...] = jnp.zeros_like(total)
    count = jnp.minimum(live[0], 64)

    def pick(seen, mask, f):
        chosen = jnp.where(mask, seen[32 * f : 32 * f + 32], 0.0)
        return chosen[0:8] + chosen[8:16] + (chosen[16:24] + chosen[24:32])

    def step(it, carry):
        block = pairs[pl.ds(pl.multiple_of(it * 8, 8), 8), :]
        index_p = lanes(block, (0, 2, 4, 6))
        index_q = lanes(block, (1, 3, 5, 7))
        low_p = (index_p & 127) + ((index_p >> 12) << 7)
        row_p = (index_p >> 7) & 31
        is_ghost = index_q >= 8192
        wrapped = index_q - 8192
        low_q = (index_q & 127) + (jnp.where(is_ghost, wrapped >> 10, index_q >> 12) << 7)
        row_q = jnp.where(is_ghost, 32 + ((wrapped >> 7) & 7), (index_q >> 7) & 31)
        hot_p = as_bf16(one_hot(256, low_p))
        hot_q = as_bf16(one_hot(256, low_q))
        seen_p = jnp.dot(
            table[...], jnp.concatenate([hot_p, hot_p], axis=0), preferred_element_type=F32
        )
        seen_q = jnp.dot(
            seconds[...], jnp.concatenate([hot_q, hot_q], axis=0), preferred_element_type=F32
        )
        mask_p = one_hot(32, row_p)
        mask_q = one_hot(32, row_q)
        mask_g = one_hot(8, row_q - 32)
        first, second = [], []
        for f in range(10):
            first.append(jnp.sum(pick(seen_p, mask_p, f), axis=0, keepdims=True))
            beyond = jnp.where(mask_g, seen_q[320 + 8 * f : 328 + 8 * f], 0.0)
            second.append(jnp.sum(pick(seen_q, mask_q, f) + beyond, axis=0, keepdims=True))
        force, twist = contact_terms(first, second)
        lane = lax.broadcasted_iota(jnp.int32, (1, span), 1)
        keep = jnp.where(4 * it + (lane >> 7) < count, 1.0, 0.0)
        to_p = [keep * v for v in force] + [keep * first[9] * v for v in twist]
        to_q = [-keep * v for v in force] + [keep * second[9] * v for v in twist]
        spread_p = jnp.concatenate([jnp.where(mask_p, v, 0.0) for v in to_p], axis=0)
        spread_q = jnp.concatenate(
            [jnp.where(mask_q, v, 0.0) for v in to_q] + [jnp.where(mask_g, v, 0.0) for v in to_q],
            axis=0,
        )
        high_p, rest_p = split(spread_p)
        high_q, rest_q = split(spread_q)
        sum_p = dot_nt(
            jnp.concatenate([high_p, rest_p], axis=1), jnp.concatenate([hot_p, hot_p], axis=1)
        )
        sum_q = dot_nt(
            jnp.concatenate([high_q, rest_q], axis=1), jnp.concatenate([hot_q, hot_q], axis=1)
        )
        total[0:192, :] += sum_p + sum_q[0:192]
        total[192:240, :] += sum_q[192:240]
        return carry

    lax.fori_loop(0, (count + 3) // 4, step, 0)
    for f in range(6):
        returned[f, 0:8, :] = total[192 + 8 * f : 200 + 8 * f, 0:128]
        returned[f, 8:16, :] = total[192 + 8 * f : 200 + 8 * f, 128:256]
    for f in range(3):
        for k in range(64):
            at = slice(128 * k, 128 * k + 128)
            side = slice(128 * (k // 32), 128 * (k // 32) + 128)
            row = 32 * f + k % 32
            force_out[f : f + 1, at] = total[row : row + 1, side] + drag[f : f + 1, at]
            twist_out[f : f + 1, at] = total[96 + row : 97 + row, side]


def border_kernel(returned, force_in, twist_in, force_out, twist_out):
    for f in range(3):
        for k in range(16):
            at = slice(128 * k, 128 * k + 128)
            force_out[f : f + 1, at] = force_in[f : f + 1, at] + returned[f, k : k + 1, :]
            twist_out[f : f + 1, at] = twist_in[f : f + 1, at] + returned[3 + f, k : k + 1, :]


def next_row(x):
    return pltpu.roll(x, x.shape[0] - 1, 0)


def last_row(x):
    return pltpu.roll(x, 1, 0)


def rows_kernel(place, own, even_side, odd_side, wide):
    even = (place[1] & 1) == 0
    sub = lax.broadcasted_iota(jnp.int32, (8, 128), 0)

    def extend(f, layer):
        e, o = even_side[f, layer], odd_side[f, layer]
        after = jnp.where(even, e, o)
        before = jnp.where(even, o, e)
        return jnp.concatenate([own[f, layer], jnp.where(sub < 4, after, before)], axis=0)

    for layer in range(2):
        wide[0, layer] = extend(0, layer)
        wide[1, layer] = extend(1, layer)
        my = extend(2, layer)
        wide[2, layer] = extend(3, layer) + 0.5 * (next_row(my) - last_row(my))


SHIFT = 3.0


def krylov_kernel(place, own, side_a, side_b, far_c, far_d, sums, basis):
    gx, gy = place[0], place[1]
    even = (gx & 1) == 0

    def layers(f):
        a = [side_a[f, s] for s in range(2)]
        b = [side_b[f, s] for s in range(2)]
        c = [far_c[f, s] for s in range(2)]
        d = [far_d[f, s] for s in range(2)]
        pick = lambda u, v: [jnp.where(even, x, y) for x, y in zip(u, v)]
        return pick(c, d) + pick(b, a) + [own[f, 0], own[f, 1]] + pick(a, b) + pick(d, c)

    mx, por, part = layers(0), layers(1), layers(2)
    row = lax.broadcasted_iota(jnp.int32, (16, 128), 0)
    lane = lax.broadcasted_iota(jnp.int32, (16, 128), 1)
    inside_y = (row < 8) | ((row < 12) & (gy < 7)) | ((row >= 12) & (gy > 0))

    def inside(l):
        x = gx * 2 + (l - 4)
        return inside_y & (x >= 0) & (x < 64)

    masks = [inside(l) for l in range(10)]
    zplus = lambda x: jnp.where(lane == 127, 0.0, pltpu.roll(x, 127, 1))
    zminus = lambda x: jnp.where(lane == 0, 0.0, pltpu.roll(x, 1, 1))
    half = [0.5 * p for p in por]
    wx = [half[l] + half[l + 1] for l in range(9)]
    wy = [h + next_row(h) for h in half]
    wy_low = [last_row(w) for w in wy]
    wz = [h + zplus(h) for h in half]
    wz_low = [h + zminus(h) for h in half]

    def apply(p, l):
        c = p[l]
        return (
            wx[l] * (c - p[l + 1])
            + wx[l - 1] * (c - p[l - 1])
            + wy[l] * (c - next_row(c))
            + wy_low[l] * (c - last_row(c))
            + wz[l] * (c - zplus(c))
            + wz_low[l] * (c - zminus(c))
        )

    v0 = {
        l: jnp.where(masks[l], part[l] + 0.5 * (mx[l + 1] - mx[l - 1]), 0.0) for l in range(1, 9)
    }
    a0 = {l: apply(v0, l) for l in range(2, 8)}
    v1 = {l: jnp.where(masks[l], a0[l] * (1.0 / SHIFT) - v0[l], 0.0) for l in a0}
    a1 = {l: apply(v1, l) for l in range(3, 7)}
    v2 = {l: jnp.where(masks[l], a1[l] * (1.0 / SHIFT) - v1[l], 0.0) for l in a1}
    a2 = {l: apply(v2, l) for l in range(4, 6)}

    def inner(p, q):
        return jnp.sum(p[4][0:8] * q[4][0:8] + p[5][0:8] * q[5][0:8], keepdims=True)

    products = [
        inner(v0, a0),
        inner(v1, a0),
        inner(v2, a0),
        inner(v1, a1),
        inner(v2, a1),
        inner(v2, a2),
        inner(v0, v0),
        inner(v1, v0),
        inner(v2, v0),
    ]
    at = lax.broadcasted_iota(jnp.int32, (8, 128), 1)
    line = jnp.zeros((8, 128), F32)
    for k, value in enumerate(products):
        line = jnp.where(at == k, value, line)
    for r in range(32):
        sums[8 * r : 8 * r + 8, :] = line
    for s in range(2):
        basis[0, s] = v0[4 + s][0:8]
        basis[1, s] = v1[4 + s][0:8]
        basis[2, s] = v2[4 + s][0:8]


def pressure_kernel(sums, basis, pressure):
    line = jnp.sum(sums[...], axis=0, keepdims=True)
    at = lax.broadcasted_iota(jnp.int32, (1, 128), 1)
    h00, h01, h02, h11, h12, h22, g0, g1, g2 = [
        jnp.sum(jnp.where(at == k, line, 0.0), axis=1, keepdims=True) for k in range(9)
    ]
    l10 = h01 / h00
    l20 = h02 / h00
    d1 = h11 - l10 * h01
    e = h12 - l10 * h02
    l21 = e / d1
    d2 = h22 - l20 * h02 - l21 * e
    y1 = g1 - l10 * g0
    y2 = g2 - l20 * g0 - l21 * y1
    c2 = y2 / d2
    c1 = y1 / d1 - l21 * c2
    c0 = g0 / h00 - l10 * c1 - l20 * c2
    for s in range(2):
        pressure[s] = c0 * basis[0, s] + c1 * basis[1, s] + c2 * basis[2, s]


def shape(*dims, dtype=F32):
    return jax.ShapeDtypeStruct(dims, dtype)


def call(kernel, out, specs, outs=None, scratch=(), cost=None, **more):
    return pl.pallas_call(
        kernel,
        out_shape=out,
        in_specs=specs,
        out_specs=outs if outs is not None else jax.tree.map(lambda _: VMEM_SPEC, out),
        scratch_shapes=scratch,
        compiler_params=PARAMS,
        cost_estimate=cost,
        **more,
    )


def swaps(count):
    even = [(i, i ^ 1) for i in range(count)]
    odd = [(i, ((i + 1) ^ 1) - 1) for i in range(1, count - 1)]
    return even, odd


def per_device(pos, vel, spin, radius, cell, pairs, live, fluid):
    place = jnp.stack([lax.axis_index("gx"), lax.axis_index("gy")]).astype(jnp.int32)
    radius = radius.reshape(64, 128)
    cell = cell.reshape(64, 128)
    pairs = pairs.reshape(128, 128)
    fluid = fluid.reshape(48, 128)
    even_x, odd_x = swaps(32)
    even_y, odd_y = swaps(8)

    fields, drag = call(
        deposit_kernel, (shape(4, 2, 8, 128), shape(3, 8192)), [VMEM_SPEC] * 4
    )(vel, radius, cell, fluid)
    table, border = call(
        table_kernel,
        (shape(320, 512, dtype=BF16), shape(10, 16, 128)),
        [SMEM_SPEC] + [VMEM_SPEC] * 5,
    )(place, pos, vel, spin, radius, cell)

    even_side = lax.ppermute(fields, "gy", even_y)
    odd_side = lax.ppermute(fields, "gy", odd_y)
    ghost = lax.ppermute(border, "gx", [(i, i + 1) for i in range(31)])
    wide = call(rows_kernel, shape(3, 2, 16, 128), [SMEM_SPEC] + [VMEM_SPEC] * 3)(
        place, fields, even_side, odd_side
    )
    side_a = lax.ppermute(wide, "gx", even_x)
    side_b = lax.ppermute(wide, "gx", odd_x)
    far_c = lax.ppermute(side_a, "gx", odd_x)
    far_d = lax.ppermute(side_b, "gx", even_x)
    sums, basis = call(
        krylov_kernel, (shape(256, 128), shape(3, 2, 8, 128)), [SMEM_SPEC] + [VMEM_SPEC] * 5
    )(place, wide, side_a, side_b, far_c, far_d)
    every = lax.all_to_all(sums, BOTH, 0, 0, tiled=True)

    force, twist, back = call(
        contact_kernel,
        (shape(3, 8192), shape(3, 8192), shape(6, 16, 128)),
        [SMEM_SPEC] + [VMEM_SPEC] * 4,
        scratch=[pltpu.VMEM((400, 512), BF16), pltpu.VMEM((240, 256), F32)],
        cost=pl.CostEstimate(flops=5 * 10**9, bytes_accessed=10**6, transcendentals=0),
    )(live, pairs, table, ghost, drag)
    returned = lax.ppermute(back, "gx", [(i + 1, i) for i in range(31)])
    head = pl.BlockSpec((3, 2048), lambda i: (0, 0))
    force, twist = call(
        border_kernel,
        (shape(3, 8192), shape(3, 8192)),
        [pl.BlockSpec((6, 16, 128), lambda i: (0, 0, 0)), head, head],
        outs=(head, head),
        grid=(1,),
        input_output_aliases={1: 0, 2: 1},
    )(returned, force, twist)
    pressure = call(pressure_kernel, shape(2, 8, 128), [VMEM_SPEC] * 2)(every, basis)
    return force, twist, pressure


def solution(mesh):
    return jax.shard_map(
        per_device,
        mesh=mesh,
        in_specs=(
            P(None, BOTH),
            P(None, BOTH),
            P(None, BOTH),
            P(BOTH),
            P(BOTH),
            P(BOTH, None, None),
            P(BOTH),
            P(None, "gx", "gy", None),
        ),
        out_specs=(P(None, BOTH), P(None, BOTH), P("gx", "gy", None)),
        check_vma=False,
    )
```

```python
import functools

import jax
import jax.numpy as jnp
from jax import lax
from jax.experimental import pallas as pl
from jax.experimental.pallas import tpu as pltpu
from jax.sharding import PartitionSpec as P

STIFFNESS = 4.0
DAMPING = 1.0
FRICTION = 0.5
SLIP_SCALE = 0.1
DRAG_RATE = 3.0
SPHERE = 4.18879020478639

F32 = jnp.float32
BF16 = jnp.bfloat16
BOTH = ("gx", "gy")
VMEM_SPEC = pl.BlockSpec(memory_space=pltpu.VMEM)
SMEM_SPEC = pl.BlockSpec(memory_space=pltpu.SMEM)
PARAMS = pltpu.CompilerParams(vmem_limit_bytes=24 * 1024 * 1024)


def split(x):
    high = x.astype(BF16)
    return high, (x - high.astype(F32)).astype(BF16)


def one_hot(size, index):
    rows = lax.broadcasted_iota(jnp.int32, (size, index.shape[1]), 0)
    return rows == index


def hot_rows(size, index):
    rows = lax.broadcasted_iota(jnp.int32, (size, 128), 0).astype(F32).astype(BF16)
    out = []
    for k in range(index.shape[1] // 128):
        here = index[:, 128 * k : 128 * k + 128].astype(F32)
        here = jnp.broadcast_to(here, (size, 128)).astype(BF16)
        out.append(jnp.where(rows == here, jnp.ones((), BF16), jnp.zeros((), BF16)))
    return jnp.concatenate(out, axis=1)


def as_bf16(mask):
    return jnp.where(mask, 1.0, 0.0).astype(BF16)


def lanes(block, rows):
    return jnp.concatenate([block[r : r + 1, :] for r in rows], axis=1)


def dot_nt(left, right):
    return lax.dot_general(left, right, (((1,), (1,)), ((), ())), preferred_element_type=F32)


def fold(blocks):
    sub = lax.broadcasted_iota(jnp.int32, (8, 128), 0)
    for step in (4, 2, 1):
        low = (sub & step) == 0
        half = len(blocks) // 2
        blocks = [
            jnp.where(
                low,
                blocks[i] + pltpu.roll(blocks[i], 8 - step, 0),
                blocks[i + half] + pltpu.roll(blocks[i + half], step, 0),
            )
            for i in range(half)
        ]
    return blocks[0]


def tiles(x):
    return [x[:, 128 * k : 128 * k + 128] for k in range(x.shape[1] // 128)]


def halves(x):
    high = x.astype(BF16).astype(F32)
    return high, (x - high).astype(BF16).astype(F32)


def dense(ref, d, count=64):
    return jnp.concatenate(
        [ref[d : d + 1, 128 * k : 128 * k + 128] for k in range(count)], axis=0
    )


def spread(ref, v, row, masks):
    value = jnp.broadcast_to(ref[v, pl.ds(row, 1), :], (16, 128)).astype(BF16)
    return [value * m for m in masks]


def load_all(sources, targets, sems):
    copies = [
        pltpu.make_async_copy(src, dst, sems.at[k])
        for k, (src, dst) in enumerate(zip(sources, targets))
    ]
    for copy in copies:
        copy.start()
    return copies


def deposit_kernel(
    cell_in, fluid_in, radius_in, vel_in, pos_in, spin_in,
    fields, drag, cell, radius, vel, pos, spin, fluid, parts, sems,
):
    copies = load_all(
        (cell_in, fluid_in, radius_in, vel_in, pos_in, spin_in),
        (cell, fluid, radius, vel, pos, spin),
        sems,
    )
    for copy in copies[:4]:
        copy.wait()
    fluid_high, fluid_low = split(fluid[...])
    fluid_table = jnp.concatenate([fluid_high, fluid_low], axis=1)
    total = jnp.zeros((128, 128), F32)
    for g in range(8):
        rows = slice(8 * g, 8 * g + 8)
        cells = lanes(cell[rows, :], range(8))
        hot = hot_rows(128, cells & 127)
        mask = one_hot(16, cells >> 7)
        seen = jnp.dot(
            fluid_table, jnp.concatenate([hot, hot], axis=0), preferred_element_type=F32
        )
        rad = radius[rows, :]
        values = []
        for d in range(3):
            chosen = jnp.where(mask, seen[16 * d : 16 * d + 16], 0.0)
            u = fold(tiles(chosen[0:8] + chosen[8:16]))
            v = jnp.concatenate(
                [vel[d : d + 1, 1024 * g + 128 * k : 1024 * g + 128 * k + 128] for k in range(8)],
                axis=0,
            )
            force = DRAG_RATE * rad * (u - v)
            drag[d, rows, :] = force
            values.append(-force)
        values.append(SPHERE * rad * rad * rad)
        for k, value in enumerate(values):
            high, low = halves(value)
            parts[k, rows, :] = high
            parts[4 + k, rows, :] = low
        masks = tiles(as_bf16(mask))
        left = [
            jnp.concatenate([spread(parts, v, 8 * g + k, masks[k : k + 1])[0] for v in range(8)], 0)
            for k in range(8)
        ]
        total = total + dot_nt(jnp.concatenate(left, axis=1), hot)
    total = total[0:64] + total[64:128]
    lane = lax.broadcasted_iota(jnp.int32, (16, 128), 1)
    mz = total[32:48]
    up = jnp.where(lane == 127, 0.0, pltpu.roll(mz, 127, 1))
    down = jnp.where(lane == 0, 0.0, pltpu.roll(mz, 1, 1))
    out = [total[0:16], 1.0 / (1.0 + total[48:64]), total[16:32], 0.5 * (up - down)]
    for f in range(4):
        for layer in range(2):
            fields[f, layer] = out[f][8 * layer : 8 * layer + 8]
    for copy in copies[4:]:
        copy.wait()


def table_kernel(place, pos, vel, spin, radius, cell, table, border):
    cells = cell[...]
    rad = radius[...]
    corner = [
        place[0] * 2 + (cells >> 10),
        place[1] * 8 + ((cells >> 7) & 7),
        cells & 127,
    ]
    fields = [dense(pos, d) - corner[d].astype(F32) for d in range(3)]
    fields += [dense(vel, d) for d in range(3)]
    fields += [rad * dense(spin, d) for d in range(3)]
    fields += [rad]
    for f in range(10):
        high, low = split(fields[f])
        rows = pl.ds(32 * f, 32)
        table[rows, 0:128] = high[0:32]
        table[rows, 128:256] = high[32:64]
        table[rows, 256:384] = low[0:32]
        table[rows, 384:512] = low[32:64]
        border[f] = fields[f][0:16] - 1.0 if f == 0 else fields[f][0:16]


BLOCKS = 32


def first_index(block):
    index = lanes(block, range(0, 16, 2))
    return (index >> 7) & 31, (index & 127) + ((index >> 12) << 7)


def second_index(block):
    index = lanes(block, range(1, 16, 2))
    beyond = index - 8192
    row = jnp.where(beyond >= 0, 32 + ((beyond >> 7) & 7), (index >> 7) & 31)
    side = jnp.where(beyond >= 0, beyond >> 10, index >> 12)
    return row, (index & 127) + (side << 7)


def groups(live):
    return (jnp.minimum(live, BLOCKS) + 7) // 8


def pair_block(pairs, it):
    return pairs[pl.ds(pl.multiple_of(it * 16, 16), 16), :]


def gather(table, row, place, beyond):
    out = [[] for _ in range(10)]
    for part in range(2):
        here = slice(512 * part, 512 * part + 512)
        hot = hot_rows(256, place[:, here])
        mask = one_hot(32, row[:, here])
        seen = jnp.dot(table[...], jnp.concatenate([hot, hot], axis=0), preferred_element_type=F32)
        for f in range(10):
            s = jnp.where(mask, seen[32 * f : 32 * f + 32], 0.0)
            s = (s[0:8] + s[8:16]) + (s[16:24] + s[24:32])
            if beyond:
                mask_far = one_hot(8, row[:, here] - 32)
                s = s + jnp.where(mask_far, seen[320 + 8 * f : 328 + 8 * f], 0.0)
            out[f] += tiles(s)
    return [fold(x) for x in out]


def cross(a, b):
    return [
        a[1] * b[2] - a[2] * b[1],
        a[2] * b[0] - a[0] * b[2],
        a[0] * b[1] - a[1] * b[0],
    ]


def dot3(a, b):
    return a[0] * b[0] + a[1] * b[1] + a[2] * b[2]


def contact_terms(first, second):
    offset = [second[d] - first[d] for d in range(3)]
    distance = jnp.sqrt(dot3(offset, offset))
    reach = first[9] + second[9]
    inverse = 1.0 / jnp.maximum(distance, 0.25 * reach)
    normal = [o * inverse for o in offset]
    correlation = jnp.maximum(reach - distance, 0.0)
    root = jnp.sqrt(correlation)
    lever = [first[6 + d] + second[6 + d] for d in range(3)]
    turn = cross(lever, normal)
    slip = [second[3 + d] - first[3 + d] - turn[d] for d in range(3)]
    speed = dot3(slip, normal)
    push = STIFFNESS * correlation * root - DAMPING * root * speed
    tangent = [slip[d] - speed * normal[d] for d in range(3)]
    size = jnp.sqrt(dot3(tangent, tangent) + SLIP_SCALE * SLIP_SCALE)
    scale = FRICTION * jnp.abs(push) / size
    friction = [scale * t for t in tangent]
    force = [friction[d] - push * normal[d] for d in range(3)]
    twist = cross(normal, friction)
    return force, twist


def contact_kernel(live, pairs, table, ghost, parts_p, parts_q, back, first, second, full, sum_far):
    count = live[0]
    full[0:320, :] = table[...]
    pieces = [
        jnp.concatenate([ghost[f, 0:8, :], ghost[f, 8:16, :]], axis=1) for f in range(10)
    ]
    high, low = split(jnp.concatenate(pieces, axis=0))
    full[320:400, 0:256] = high
    full[320:400, 256:512] = low

    def look(it, carry):
        block = pair_block(pairs, it)
        rows = pl.ds(pl.multiple_of(it * 8, 8), 8)
        p = gather(table, *first_index(block), False)
        q = gather(full, *second_index(block), True)
        for f in range(10):
            first[f, rows, :] = p[f]
            second[f, rows, :] = q[f]
        return carry

    lax.fori_loop(0, groups(count), look, 0)
    p = [first[f] for f in range(10)]
    q = [second[f] for f in range(10)]
    force, twist = contact_terms(p, q)
    keep = lax.broadcasted_iota(jnp.int32, (BLOCKS, 128), 0) < count
    to_p = force + [p[9] * v for v in twist]
    to_q = [-v for v in force] + [q[9] * v for v in twist]
    for k in range(6):
        for parts, values in ((parts_p, to_p), (parts_q, to_q)):
            high, low = halves(jnp.where(keep, values[k], 0.0))
            parts[k] = high
            parts[6 + k] = low
    sum_far[...] = jnp.zeros_like(sum_far)

    def step(it, carry):
        row, place = second_index(pair_block(pairs, it))
        hot = hot_rows(256, place)
        far = as_bf16(one_hot(16, row - 32))
        left = [
            jnp.concatenate(
                sum([spread(parts_q, v, it * 8 + k, [m]) for v in range(12)], []), axis=0
            )
            for k, m in enumerate(tiles(far))
        ]
        sum_far[...] += dot_nt(jnp.concatenate(left, axis=1), hot)
        return carry

    lax.fori_loop(0, groups(count), step, 0)
    for f in range(6):
        rows = sum_far[16 * f : 16 * f + 8, :] + sum_far[96 + 16 * f : 104 + 16 * f, :]
        back[f, 0:8, :] = rows[:, 0:128]
        back[f, 8:16, :] = rows[:, 128:256]


def own_kernel(live, pairs, parts_p, parts_q, total, sum_p, sum_q):
    sum_p[...] = jnp.zeros_like(sum_p)
    sum_q[...] = jnp.zeros_like(sum_q)

    def step(it, carry):
        block = pair_block(pairs, it)
        for index, parts, sums in (
            (first_index, parts_p, sum_p),
            (second_index, parts_q, sum_q),
        ):
            row, place = index(block)
            hot = hot_rows(256, place)
            mask = as_bf16(one_hot(32, row))
            left = [
                jnp.concatenate(
                    sum([spread(parts, v, it * 8 + k, [m[0:16], m[16:32]]) for v in range(12)], []),
                    axis=0,
                )
                for k, m in enumerate(tiles(mask))
            ]
            sums[...] += dot_nt(jnp.concatenate(left, axis=1), hot)
        return carry

    lax.fori_loop(0, groups(live[0]), step, 0)
    for f in range(6):
        rows = slice(32 * f, 32 * f + 32)
        rest = slice(192 + 32 * f, 224 + 32 * f)
        own = (sum_p[rows, :] + sum_p[rest, :]) + (sum_q[rows, :] + sum_q[rest, :])
        total[f, 0:32, :] = own[:, 0:128]
        total[f, 32:64, :] = own[:, 128:256]


def finish_kernel(total, returned, drag, sums, basis, force_out, twist_out, pressure):
    solve(sums, basis, pressure)
    for f in range(3):
        for g in range(8):
            rows = slice(8 * g, 8 * g + 8)
            force = total[f, rows, :] + drag[f, rows, :]
            twist = total[3 + f, rows, :]
            if g < 2:
                force = force + returned[f, rows, :]
                twist = twist + returned[3 + f, rows, :]
            for k in range(8):
                at = slice(1024 * g + 128 * k, 1024 * g + 128 * k + 128)
                force_out[f : f + 1, at] = force[k : k + 1]
                twist_out[f : f + 1, at] = twist[k : k + 1]


def next_row(x):
    return pltpu.roll(x, x.shape[0] - 1, 0)


def last_row(x):
    return pltpu.roll(x, 1, 0)


def rows_kernel(place, own, even_side, odd_side, near, slim):
    even = (place[1] & 1) == 0
    sub = lax.broadcasted_iota(jnp.int32, (8, 128), 0)

    def extend(f, layer):
        e, o = even_side[f, layer], odd_side[f, layer]
        after = jnp.where(even, e, o)
        before = jnp.where(even, o, e)
        return jnp.concatenate([own[f, layer], jnp.where(sub < 4, after, before)], axis=0)

    def put(f, layer, x):
        near[32 * f + 16 * layer : 32 * f + 16 * layer + 16, :] = x

    for layer in range(2):
        mx = extend(0, layer)
        my = extend(2, layer)
        part = extend(3, layer) + 0.5 * (next_row(my) - last_row(my))
        put(0, layer, mx)
        put(1, layer, extend(1, layer))
        put(2, layer, part)
        slim[0, layer] = mx[0:8]
        slim[1, layer] = mx[8:16]
        slim[2, layer] = own[1, layer]
        slim[3, layer] = part[0:8]


SHIFT = 3.0


def krylov_kernel(place, own, near_a, near_b, far_a, far_b, sums, basis):
    gx, gy = place[0], place[1]
    up_a = (gx & 1) == 0
    far_up_a = (gx & 2) == 0
    blank = jnp.zeros((8, 128), F32)

    def layers(f):
        def far(ref, s):
            if f == 0:
                return jnp.concatenate([ref[0, s], ref[1, s]], axis=0)
            return jnp.concatenate([ref[1 + f, s], blank], axis=0)

        pick = lambda cond, u, v: [jnp.where(cond, x, y) for x, y in zip(u, v)]
        near = lambda ref, s: ref[32 * f + 16 * s : 32 * f + 16 * s + 16, :]
        a = [near(near_a, s) for s in range(2)]
        b = [near(near_b, s) for s in range(2)]
        c = [far(far_a, s) for s in range(2)]
        d = [far(far_b, s) for s in range(2)]
        return (
            pick(far_up_a, d, c)
            + pick(up_a, b, a)
            + [near(own, 0), near(own, 1)]
            + pick(up_a, a, b)
            + pick(far_up_a, c, d)
        )

    mx, por, part = layers(0), layers(1), layers(2)
    row = lax.broadcasted_iota(jnp.int32, (16, 128), 0)
    lane = lax.broadcasted_iota(jnp.int32, (16, 128), 1)
    inside_y = (row < 8) | ((row < 12) & (gy < 7)) | ((row >= 12) & (gy > 0))

    def inside(l):
        x = gx * 2 + (l - 4)
        return inside_y & (x >= 0) & (x < 64)

    masks = [inside(l) for l in range(10)]
    zplus = lambda x: jnp.where(lane == 127, 0.0, pltpu.roll(x, 127, 1))
    zminus = lambda x: jnp.where(lane == 0, 0.0, pltpu.roll(x, 1, 1))
    half = [0.5 * p for p in por]
    wx = [half[l] + half[l + 1] for l in range(9)]
    wy = [h + next_row(h) for h in half]
    wy_low = [last_row(w) for w in wy]
    wz = [h + zplus(h) for h in half]
    wz_low = [h + zminus(h) for h in half]

    def apply(p, l):
        c = p[l]
        return (
            wx[l] * (c - p[l + 1])
            + wx[l - 1] * (c - p[l - 1])
            + wy[l] * (c - next_row(c))
            + wy_low[l] * (c - last_row(c))
            + wz[l] * (c - zplus(c))
            + wz_low[l] * (c - zminus(c))
        )

    v0 = {
        l: jnp.where(masks[l], part[l] + 0.5 * (mx[l + 1] - mx[l - 1]), 0.0) for l in range(1, 9)
    }
    a0 = {l: apply(v0, l) for l in range(2, 8)}
    v1 = {l: jnp.where(masks[l], a0[l] * (1.0 / SHIFT) - v0[l], 0.0) for l in a0}
    a1 = {l: apply(v1, l) for l in range(3, 7)}
    v2 = {l: jnp.where(masks[l], a1[l] * (1.0 / SHIFT) - v1[l], 0.0) for l in a1}
    a2 = {l: apply(v2, l) for l in range(4, 6)}

    def inner(p, q):
        return p[4][0:8] * q[4][0:8] + p[5][0:8] * q[5][0:8]

    products = [
        inner(v0, a0),
        inner(v1, a0),
        inner(v2, a0),
        inner(v1, a1),
        inner(v2, a1),
        inner(v2, a2),
        inner(v0, v0),
        inner(v1, v0),
    ]
    at = lax.broadcasted_iota(jnp.int32, (8, 128), 1)
    sub = lax.broadcasted_iota(jnp.int32, (8, 128), 0)
    eight = jnp.sum(fold(products), axis=1, keepdims=True)
    ninth = jnp.sum(inner(v2, v0), keepdims=True)
    line = jnp.sum(jnp.where(at == sub, eight, 0.0), axis=0, keepdims=True)
    line = line + jnp.where(at[0:1] == 8, ninth, 0.0)
    sums[...] = jnp.broadcast_to(line, (256, 128))
    for s in range(2):
        basis[0, s] = v0[4 + s][0:8]
        basis[1, s] = v1[4 + s][0:8]
        basis[2, s] = v2[4 + s][0:8]


def solve(sums, basis, pressure):
    line = jnp.sum(sums[...], axis=0, keepdims=True)
    at = lax.broadcasted_iota(jnp.int32, (1, 128), 1)
    h00, h01, h02, h11, h12, h22, g0, g1, g2 = [
        jnp.sum(jnp.where(at == k, line, 0.0), axis=1, keepdims=True) for k in range(9)
    ]
    l10 = h01 / h00
    l20 = h02 / h00
    d1 = h11 - l10 * h01
    e = h12 - l10 * h02
    l21 = e / d1
    d2 = h22 - l20 * h02 - l21 * e
    y1 = g1 - l10 * g0
    y2 = g2 - l20 * g0 - l21 * y1
    c2 = y2 / d2
    c1 = y1 / d1 - l21 * c2
    c0 = g0 / h00 - l10 * c1 - l20 * c2
    for s in range(2):
        pressure[s] = c0 * basis[0, s] + c1 * basis[1, s] + c2 * basis[2, s]


def shape(*dims, dtype=F32):
    return jax.ShapeDtypeStruct(dims, dtype)


def call(kernel, out, specs, outs=None, scratch=(), cost=None, **more):
    return pl.pallas_call(
        kernel,
        out_shape=out,
        in_specs=specs,
        out_specs=outs if outs is not None else jax.tree.map(lambda _: VMEM_SPEC, out),
        scratch_shapes=scratch,
        compiler_params=PARAMS,
        cost_estimate=cost,
        **more,
    )


def work(us):
    return pl.CostEstimate(flops=us * 10**9, bytes_accessed=0, transcendentals=0)


def in_hbm(*arrays):
    return [pltpu.with_memory_space_constraint(x, pltpu.HBM) for x in arrays]


def swaps(count):
    even = [(i, i ^ 1) for i in range(count)]
    odd = [(i, ((i + 1) ^ 1) - 1) for i in range(1, count - 1)]
    return even, odd


def per_device(pos, vel, spin, radius, cell, pairs, live, fluid):
    place = jnp.stack([lax.axis_index("gx"), lax.axis_index("gy")]).astype(jnp.int32)
    radius = radius.reshape(64, 128)
    cell = cell.reshape(64, 128)
    pairs = pairs.reshape(128, 128)
    fluid = fluid.reshape(48, 128)
    even_x, odd_x = swaps(32)
    even_y, odd_y = swaps(8)

    hbm = pl.BlockSpec(memory_space=pltpu.HBM)
    flat = shape(64, 128)
    fields, drag, cell, radius, vel, pos, spin = call(
        deposit_kernel,
        (
            shape(4, 2, 8, 128),
            shape(3, 64, 128),
            shape(64, 128, dtype=jnp.int32),
            flat,
            shape(3, 8192),
            shape(3, 8192),
            shape(3, 8192),
        ),
        [hbm] * 6,
        scratch=[
            pltpu.VMEM((48, 128), F32),
            pltpu.VMEM((8, 64, 128), F32),
            pltpu.SemaphoreType.DMA((6,)),
        ],
    )(*in_hbm(cell, fluid, radius, vel, pos, spin))
    table, border = call(
        table_kernel,
        (shape(320, 512, dtype=BF16), shape(10, 16, 128)),
        [SMEM_SPEC] + [VMEM_SPEC] * 5,
    )(place, pos, vel, spin, radius, cell)

    even_side = lax.ppermute(fields, "gy", even_y)
    odd_side = lax.ppermute(fields, "gy", odd_y)
    near, slim = call(
        rows_kernel,
        (shape(96, 128), shape(4, 2, 8, 128)),
        [SMEM_SPEC] + [VMEM_SPEC] * 3,
    )(place, fields, even_side, odd_side)
    near, slim, border = lax.optimization_barrier((near, slim, border))
    near_b = lax.ppermute(near, "gx", odd_x)
    far_b = lax.ppermute(slim, "gx", [(i, ((i + 2) ^ 2) - 2) for i in range(2, 30)])
    near_a = lax.ppermute(near, "gx", even_x)
    far_a = lax.ppermute(slim, "gx", [(i, i ^ 2) for i in range(32)])
    ghost = lax.ppermute(border, "gx", [(i, i + 1) for i in range(31)])
    sums, basis = call(
        krylov_kernel, (shape(256, 128), shape(3, 2, 8, 128)), [SMEM_SPEC] + [VMEM_SPEC] * 5, cost=work(8),
    )(place, near, near_a, near_b, far_a, far_b)
    every = lax.all_to_all(sums, BOTH, 0, 0, tiled=True)

    table, sums = lax.optimization_barrier((table, sums))
    sums_384 = pltpu.VMEM((384, 256), F32)
    found = pltpu.VMEM((10, BLOCKS, 128), F32)
    twelve = shape(12, BLOCKS, 128)
    parts_p, parts_q, back = call(
        contact_kernel,
        (twelve, twelve, shape(6, 16, 128)),
        [SMEM_SPEC] + [VMEM_SPEC] * 3,
        scratch=[found, found, pltpu.VMEM((400, 512), BF16), pltpu.VMEM((192, 256), F32)],
        cost=work(2),
    )(live, pairs, table, ghost)
    returned = lax.ppermute(back, "gx", [(i + 1, i) for i in range(31)])
    total = call(
        own_kernel,
        shape(6, 64, 128),
        [SMEM_SPEC] + [VMEM_SPEC] * 3,
        scratch=[sums_384, sums_384],
        cost=work(1),
    )(live, pairs, parts_p, parts_q)
    return call(
        finish_kernel,
        (shape(3, 8192), shape(3, 8192), shape(2, 8, 128)),
        [VMEM_SPEC] * 5,
    )(total, returned, drag, every, basis)


def solution(mesh):
    return jax.shard_map(
        per_device,
        mesh=mesh,
        in_specs=(
            P(None, BOTH),
            P(None, BOTH),
            P(None, BOTH),
            P(BOTH),
            P(BOTH),
            P(BOTH, None, None),
            P(BOTH),
            P(None, "gx", "gy", None),
        ),
        out_specs=(P(None, BOTH), P(None, BOTH), P("gx", "gy", None)),
        check_vma=False,
    )
```

```python
import functools

import jax
import jax.numpy as jnp
from jax import lax
from jax.experimental import pallas as pl
from jax.experimental.pallas import tpu as pltpu
from jax.sharding import PartitionSpec as P

STIFFNESS = 4.0
DAMPING = 1.0
FRICTION = 0.5
SLIP_SCALE = 0.1
DRAG_RATE = 3.0
SPHERE = 4.18879020478639

F32 = jnp.float32
BF16 = jnp.bfloat16
BOTH = ("gx", "gy")
VMEM_SPEC = pl.BlockSpec(memory_space=pltpu.VMEM)
SMEM_SPEC = pl.BlockSpec(memory_space=pltpu.SMEM)
PARAMS = pltpu.CompilerParams(vmem_limit_bytes=24 * 1024 * 1024)


def split(x):
    high = x.astype(BF16)
    return high, (x - high.astype(F32)).astype(BF16)


def one_hot(size, index):
    rows = lax.broadcasted_iota(jnp.int32, (size, index.shape[1]), 0)
    return rows == index


def hot_rows(size, index):
    rows = lax.broadcasted_iota(jnp.int32, (size, 128), 0).astype(F32).astype(BF16)
    out = []
    for k in range(index.shape[1] // 128):
        here = index[:, 128 * k : 128 * k + 128].astype(F32)
        here = jnp.broadcast_to(here, (size, 128)).astype(BF16)
        out.append(jnp.where(rows == here, jnp.ones((), BF16), jnp.zeros((), BF16)))
    return jnp.concatenate(out, axis=1)


def as_bf16(mask):
    return jnp.where(mask, 1.0, 0.0).astype(BF16)


def lanes(block, rows):
    return jnp.concatenate([block[r : r + 1, :] for r in rows], axis=1)


def dot_nt(left, right):
    return lax.dot_general(left, right, (((1,), (1,)), ((), ())), preferred_element_type=F32)


def fold(blocks):
    sub = lax.broadcasted_iota(jnp.int32, (8, 128), 0)
    for step in (4, 2, 1):
        low = (sub & step) == 0
        half = len(blocks) // 2
        blocks = [
            jnp.where(
                low,
                blocks[i] + pltpu.roll(blocks[i], 8 - step, 0),
                blocks[i + half] + pltpu.roll(blocks[i + half], step, 0),
            )
            for i in range(half)
        ]
    return blocks[0]


def tiles(x):
    return [x[:, 128 * k : 128 * k + 128] for k in range(x.shape[1] // 128)]


def halves(x):
    high = x.astype(BF16).astype(F32)
    return high, (x - high).astype(BF16).astype(F32)


def dense(ref, d, count=64):
    return jnp.concatenate(
        [ref[d : d + 1, 128 * k : 128 * k + 128] for k in range(count)], axis=0
    )


def spread(ref, v, row, masks):
    value = jnp.broadcast_to(ref[v, pl.ds(row, 1), :], (16, 128)).astype(BF16)
    return [value * m for m in masks]


def load_all(sources, targets, sems):
    copies = [
        pltpu.make_async_copy(src, dst, sems.at[k])
        for k, (src, dst) in enumerate(zip(sources, targets))
    ]
    for copy in copies:
        copy.start()
    return copies


def deposit_kernel(
    cell_in, fluid_in, radius_in, vel_in, pos_in, spin_in,
    fields, drag, cell, radius, vel, pos, spin, fluid, parts, sems,
):
    copies = load_all(
        (cell_in, fluid_in, radius_in, vel_in, pos_in, spin_in),
        (cell, fluid, radius, vel, pos, spin),
        sems,
    )
    for copy in copies[:2]:
        copy.wait()
    fluid_high, fluid_low = split(fluid[...])
    fluid_table = jnp.concatenate([fluid_high, fluid_low], axis=1)
    total = jnp.zeros((128, 128), F32)
    for g in range(8):
        rows = slice(8 * g, 8 * g + 8)
        cells = lanes(cell[rows, :], range(8))
        hot = hot_rows(128, cells & 127)
        mask = one_hot(16, cells >> 7)
        seen = jnp.dot(
            fluid_table, jnp.concatenate([hot, hot], axis=0), preferred_element_type=F32
        )
        if g == 0:
            for copy in copies[2:4]:
                copy.wait()
        rad = radius[rows, :]
        values = []
        for d in range(3):
            chosen = jnp.where(mask, seen[16 * d : 16 * d + 16], 0.0)
            u = fold(tiles(chosen[0:8] + chosen[8:16]))
            v = jnp.concatenate(
                [vel[d : d + 1, 1024 * g + 128 * k : 1024 * g + 128 * k + 128] for k in range(8)],
                axis=0,
            )
            force = DRAG_RATE * rad * (u - v)
            drag[d, rows, :] = force
            values.append(-force)
        values.append(SPHERE * rad * rad * rad)
        for k, value in enumerate(values):
            high, low = halves(value)
            parts[k, rows, :] = high
            parts[4 + k, rows, :] = low
        masks = tiles(as_bf16(mask))
        left = [
            jnp.concatenate([spread(parts, v, 8 * g + k, masks[k : k + 1])[0] for v in range(8)], 0)
            for k in range(8)
        ]
        total = total + dot_nt(jnp.concatenate(left, axis=1), hot)
    total = total[0:64] + total[64:128]
    lane = lax.broadcasted_iota(jnp.int32, (16, 128), 1)
    mz = total[32:48]
    up = jnp.where(lane == 127, 0.0, pltpu.roll(mz, 127, 1))
    down = jnp.where(lane == 0, 0.0, pltpu.roll(mz, 1, 1))
    out = [total[0:16], 1.0 / (1.0 + total[48:64]), total[16:32], 0.5 * (up - down)]
    for f in range(4):
        for layer in range(2):
            fields[f, layer] = out[f][8 * layer : 8 * layer + 8]
    for copy in copies[4:]:
        copy.wait()


def table_kernel(pos, vel, spin, radius, cell, table, border):
    place = (lax.axis_index("gx"), lax.axis_index("gy"))
    cells = cell[...]
    rad = radius[...]
    corner = [
        place[0] * 2 + (cells >> 10),
        place[1] * 8 + ((cells >> 7) & 7),
        cells & 127,
    ]
    fields = [dense(pos, d) - corner[d].astype(F32) for d in range(3)]
    fields += [dense(vel, d) for d in range(3)]
    fields += [rad * dense(spin, d) for d in range(3)]
    fields += [rad]
    for f in range(10):
        high, low = split(fields[f])
        rows = pl.ds(32 * f, 32)
        table[rows, 0:128] = high[0:32]
        table[rows, 128:256] = high[32:64]
        table[rows, 256:384] = low[0:32]
        table[rows, 384:512] = low[32:64]
        border[f] = fields[f][0:16] - 1.0 if f == 0 else fields[f][0:16]


BLOCKS = 32


def first_index(block):
    index = lanes(block, range(0, 16, 2))
    return (index >> 7) & 31, (index & 127) + ((index >> 12) << 7)


def second_index(block):
    index = lanes(block, range(1, 16, 2))
    beyond = index - 8192
    row = jnp.where(beyond >= 0, 32 + ((beyond >> 7) & 7), (index >> 7) & 31)
    side = jnp.where(beyond >= 0, beyond >> 10, index >> 12)
    return row, (index & 127) + (side << 7)


def groups(live):
    return (jnp.minimum(live, BLOCKS) + 7) // 8


def pair_block(pairs, it):
    return pairs[pl.ds(pl.multiple_of(it * 16, 16), 16), :]


def gather(table, row, place, beyond):
    out = [[] for _ in range(10)]
    for part in range(2):
        here = slice(512 * part, 512 * part + 512)
        hot = hot_rows(256, place[:, here])
        mask = one_hot(32, row[:, here])
        seen = jnp.dot(table[...], jnp.concatenate([hot, hot], axis=0), preferred_element_type=F32)
        for f in range(10):
            s = jnp.where(mask, seen[32 * f : 32 * f + 32], 0.0)
            s = (s[0:8] + s[8:16]) + (s[16:24] + s[24:32])
            if beyond:
                mask_far = one_hot(8, row[:, here] - 32)
                s = s + jnp.where(mask_far, seen[320 + 8 * f : 328 + 8 * f], 0.0)
            out[f] += tiles(s)
    return [fold(x) for x in out]


def cross(a, b):
    return [
        a[1] * b[2] - a[2] * b[1],
        a[2] * b[0] - a[0] * b[2],
        a[0] * b[1] - a[1] * b[0],
    ]


def dot3(a, b):
    return a[0] * b[0] + a[1] * b[1] + a[2] * b[2]


def contact_terms(first, second):
    offset = [second[d] - first[d] for d in range(3)]
    distance = jnp.sqrt(dot3(offset, offset))
    reach = first[9] + second[9]
    inverse = 1.0 / jnp.maximum(distance, 0.25 * reach)
    normal = [o * inverse for o in offset]
    correlation = jnp.maximum(reach - distance, 0.0)
    root = jnp.sqrt(correlation)
    lever = [first[6 + d] + second[6 + d] for d in range(3)]
    turn = cross(lever, normal)
    slip = [second[3 + d] - first[3 + d] - turn[d] for d in range(3)]
    speed = dot3(slip, normal)
    push = STIFFNESS * correlation * root - DAMPING * root * speed
    tangent = [slip[d] - speed * normal[d] for d in range(3)]
    size = jnp.sqrt(dot3(tangent, tangent) + SLIP_SCALE * SLIP_SCALE)
    scale = FRICTION * jnp.abs(push) / size
    friction = [scale * t for t in tangent]
    force = [friction[d] - push * normal[d] for d in range(3)]
    twist = cross(normal, friction)
    return force, twist


def contact_kernel(
    live, pairs, table, ghost,
    parts_p, parts_q, back, total, first, second, full, sum_far, sum_p, sum_q,
):
    count = live[0]
    full[0:320, :] = table[...]
    pieces = [
        jnp.concatenate([ghost[f, 0:8, :], ghost[f, 8:16, :]], axis=1) for f in range(10)
    ]
    high, low = split(jnp.concatenate(pieces, axis=0))
    full[320:400, 0:256] = high
    full[320:400, 256:512] = low

    def look(it, carry):
        block = pair_block(pairs, it)
        rows = pl.ds(pl.multiple_of(it * 8, 8), 8)
        p = gather(table, *first_index(block), False)
        q = gather(full, *second_index(block), True)
        for f in range(10):
            first[f, rows, :] = p[f]
            second[f, rows, :] = q[f]
        return carry

    lax.fori_loop(0, groups(count), look, 0)
    p = [first[f] for f in range(10)]
    q = [second[f] for f in range(10)]
    force, twist = contact_terms(p, q)
    keep = lax.broadcasted_iota(jnp.int32, (BLOCKS, 128), 0) < count
    to_p = force + [p[9] * v for v in twist]
    to_q = [-v for v in force] + [q[9] * v for v in twist]
    for k in range(6):
        for parts, values in ((parts_p, to_p), (parts_q, to_q)):
            high, low = halves(jnp.where(keep, values[k], 0.0))
            parts[k] = high
            parts[6 + k] = low
    sum_far[...] = jnp.zeros_like(sum_far)

    def step(it, carry):
        row, place = second_index(pair_block(pairs, it))
        hot = hot_rows(256, place)
        far = as_bf16(one_hot(16, row - 32))
        left = [
            jnp.concatenate(
                sum([spread(parts_q, v, it * 8 + k, [m]) for v in range(12)], []), axis=0
            )
            for k, m in enumerate(tiles(far))
        ]
        sum_far[...] += dot_nt(jnp.concatenate(left, axis=1), hot)
        return carry

    lax.fori_loop(0, groups(count), step, 0)
    for f in range(6):
        rows = sum_far[16 * f : 16 * f + 8, :] + sum_far[96 + 16 * f : 104 + 16 * f, :]
        back[f, 0:8, :] = rows[:, 0:128]
        back[f, 8:16, :] = rows[:, 128:256]

    @pl.when(early())
    def _():
        own_sums(live, pairs, parts_p, parts_q, total, sum_p, sum_q)


def early():
    gx = lax.axis_index("gx")
    return (gx > 0) & ((gx & 7) == 0)


def own_sums(live, pairs, parts_p, parts_q, total, sum_p, sum_q):
    sum_p[...] = jnp.zeros_like(sum_p)
    sum_q[...] = jnp.zeros_like(sum_q)

    def step(it, carry):
        block = pair_block(pairs, it)
        for index, parts, sums in (
            (first_index, parts_p, sum_p),
            (second_index, parts_q, sum_q),
        ):
            row, place = index(block)
            hot = hot_rows(256, place)
            mask = as_bf16(one_hot(32, row))
            left = [
                jnp.concatenate(
                    sum([spread(parts, v, it * 8 + k, [m[0:16], m[16:32]]) for v in range(12)], []),
                    axis=0,
                )
                for k, m in enumerate(tiles(mask))
            ]
            sums[...] += dot_nt(jnp.concatenate(left, axis=1), hot)
        return carry

    lax.fori_loop(0, groups(live[0]), step, 0)
    for f in range(6):
        rows = slice(32 * f, 32 * f + 32)
        rest = slice(192 + 32 * f, 224 + 32 * f)
        own = (sum_p[rows, :] + sum_p[rest, :]) + (sum_q[rows, :] + sum_q[rest, :])
        total[f, 0:32, :] = own[:, 0:128]
        total[f, 32:64, :] = own[:, 128:256]


def own_kernel(live, pairs, parts_p, parts_q, before, total, sum_p, sum_q):
    @pl.when(early())
    def _():
        total[...] = before[...]

    @pl.when(jnp.logical_not(early()))
    def _():
        own_sums(live, pairs, parts_p, parts_q, total, sum_p, sum_q)


def finish_kernel(total, returned, drag, sums, basis, force_out, twist_out, pressure):
    solve(sums, basis, pressure)
    for f in range(3):
        for g in range(8):
            rows = slice(8 * g, 8 * g + 8)
            force = total[f, rows, :] + drag[f, rows, :]
            twist = total[3 + f, rows, :]
            if g < 2:
                force = force + returned[f, rows, :]
                twist = twist + returned[3 + f, rows, :]
            for k in range(8):
                at = slice(1024 * g + 128 * k, 1024 * g + 128 * k + 128)
                force_out[f : f + 1, at] = force[k : k + 1]
                twist_out[f : f + 1, at] = twist[k : k + 1]


def next_row(x):
    return pltpu.roll(x, x.shape[0] - 1, 0)


def last_row(x):
    return pltpu.roll(x, 1, 0)


def rows_kernel(own, even_side, odd_side, near, slim):
    even = (lax.axis_index("gy") & 1) == 0
    sub = lax.broadcasted_iota(jnp.int32, (8, 128), 0)

    def extend(f, layer):
        e, o = even_side[f, layer], odd_side[f, layer]
        after = jnp.where(even, e, o)
        before = jnp.where(even, o, e)
        return jnp.concatenate([own[f, layer], jnp.where(sub < 4, after, before)], axis=0)

    def put(f, layer, x):
        near[32 * f + 16 * layer : 32 * f + 16 * layer + 16, :] = x

    for layer in range(2):
        mx = extend(0, layer)
        my = extend(2, layer)
        part = extend(3, layer) + 0.5 * (next_row(my) - last_row(my))
        put(0, layer, mx)
        put(1, layer, extend(1, layer))
        put(2, layer, part)
        slim[0, layer] = mx[0:8]
        slim[1, layer] = mx[8:16]
        slim[2, layer] = own[1, layer]
        slim[3, layer] = part[0:8]


SHIFT = 3.0


def krylov_kernel(own, near_b, near_a, far_b, far_a, sums, basis):
    gx, gy = lax.axis_index("gx"), lax.axis_index("gy")
    up_a = (gx & 1) == 0
    far_up_a = (gx & 2) == 0
    blank = jnp.zeros((8, 128), F32)

    def layers(f):
        def far(ref, s):
            if f == 0:
                return jnp.concatenate([ref[0, s], ref[1, s]], axis=0)
            return jnp.concatenate([ref[1 + f, s], blank], axis=0)

        pick = lambda cond, u, v: [jnp.where(cond, x, y) for x, y in zip(u, v)]
        near = lambda ref, s: ref[32 * f + 16 * s : 32 * f + 16 * s + 16, :]
        a = [near(near_a, s) for s in range(2)]
        b = [near(near_b, s) for s in range(2)]
        c = [far(far_a, s) for s in range(2)]
        d = [far(far_b, s) for s in range(2)]
        return (
            pick(far_up_a, d, c)
            + pick(up_a, b, a)
            + [near(own, 0), near(own, 1)]
            + pick(up_a, a, b)
            + pick(far_up_a, c, d)
        )

    mx, por, part = layers(0), layers(1), layers(2)
    row = lax.broadcasted_iota(jnp.int32, (16, 128), 0)
    lane = lax.broadcasted_iota(jnp.int32, (16, 128), 1)
    inside_y = (row < 8) | ((row < 12) & (gy < 7)) | ((row >= 12) & (gy > 0))

    def inside(l):
        x = gx * 2 + (l - 4)
        return inside_y & (x >= 0) & (x < 64)

    masks = [inside(l) for l in range(10)]
    zplus = lambda x: jnp.where(lane == 127, 0.0, pltpu.roll(x, 127, 1))
    zminus = lambda x: jnp.where(lane == 0, 0.0, pltpu.roll(x, 1, 1))
    half = [0.5 * p for p in por]
    wx = [half[l] + half[l + 1] for l in range(9)]
    wy = [h + next_row(h) for h in half]
    wy_low = [last_row(w) for w in wy]
    wz = [h + zplus(h) for h in half]
    wz_low = [h + zminus(h) for h in half]

    def apply(p, l):
        c = p[l]
        return (
            wx[l] * (c - p[l + 1])
            + wx[l - 1] * (c - p[l - 1])
            + wy[l] * (c - next_row(c))
            + wy_low[l] * (c - last_row(c))
            + wz[l] * (c - zplus(c))
            + wz_low[l] * (c - zminus(c))
        )

    v0 = {
        l: jnp.where(masks[l], part[l] + 0.5 * (mx[l + 1] - mx[l - 1]), 0.0) for l in range(1, 9)
    }
    a0 = {l: apply(v0, l) for l in range(2, 8)}
    v1 = {l: jnp.where(masks[l], a0[l] * (1.0 / SHIFT) - v0[l], 0.0) for l in a0}
    a1 = {l: apply(v1, l) for l in range(3, 7)}
    v2 = {l: jnp.where(masks[l], a1[l] * (1.0 / SHIFT) - v1[l], 0.0) for l in a1}
    a2 = {l: apply(v2, l) for l in range(4, 6)}

    def inner(p, q):
        return p[4][0:8] * q[4][0:8] + p[5][0:8] * q[5][0:8]

    products = [
        inner(v0, a0),
        inner(v1, a0),
        inner(v2, a0),
        inner(v1, a1),
        inner(v2, a1),
        inner(v2, a2),
        inner(v0, v0),
        inner(v1, v0),
    ]
    at = lax.broadcasted_iota(jnp.int32, (8, 128), 1)
    sub = lax.broadcasted_iota(jnp.int32, (8, 128), 0)
    eight = jnp.sum(fold(products), axis=1, keepdims=True)
    ninth = jnp.sum(inner(v2, v0), keepdims=True)
    line = jnp.sum(jnp.where(at == sub, eight, 0.0), axis=0, keepdims=True)
    line = line + jnp.where(at[0:1] == 8, ninth, 0.0)
    sums[...] = jnp.broadcast_to(line, (256, 128))
    for s in range(2):
        basis[0, s] = v0[4 + s][0:8]
        basis[1, s] = v1[4 + s][0:8]
        basis[2, s] = v2[4 + s][0:8]


def solve(sums, basis, pressure):
    line = jnp.sum(sums[...], axis=0, keepdims=True)
    at = lax.broadcasted_iota(jnp.int32, (1, 128), 1)
    h00, h01, h02, h11, h12, h22, g0, g1, g2 = [
        jnp.sum(jnp.where(at == k, line, 0.0), axis=1, keepdims=True) for k in range(9)
    ]
    l10 = h01 / h00
    l20 = h02 / h00
    d1 = h11 - l10 * h01
    e = h12 - l10 * h02
    l21 = e / d1
    d2 = h22 - l20 * h02 - l21 * e
    y1 = g1 - l10 * g0
    y2 = g2 - l20 * g0 - l21 * y1
    c2 = y2 / d2
    c1 = y1 / d1 - l21 * c2
    c0 = g0 / h00 - l10 * c1 - l20 * c2
    for s in range(2):
        pressure[s] = c0 * basis[0, s] + c1 * basis[1, s] + c2 * basis[2, s]


def shape(*dims, dtype=F32):
    return jax.ShapeDtypeStruct(dims, dtype)


def call(kernel, out, specs, outs=None, scratch=(), cost=None, **more):
    return pl.pallas_call(
        kernel,
        out_shape=out,
        in_specs=specs,
        out_specs=outs if outs is not None else jax.tree.map(lambda _: VMEM_SPEC, out),
        scratch_shapes=scratch,
        compiler_params=PARAMS,
        cost_estimate=cost,
        **more,
    )


def work(us):
    return pl.CostEstimate(flops=us * 10**9, bytes_accessed=0, transcendentals=0)


def in_hbm(*arrays):
    return [pltpu.with_memory_space_constraint(x, pltpu.HBM) for x in arrays]


def swaps(count):
    even = [(i, i ^ 1) for i in range(count)]
    odd = [(i, ((i + 1) ^ 1) - 1) for i in range(1, count - 1)]
    return even, odd


def per_device(pos, vel, spin, radius, cell, pairs, live, fluid):
    radius = radius.reshape(64, 128)
    cell = cell.reshape(64, 128)
    pairs = pairs.reshape(128, 128)
    fluid = fluid.reshape(48, 128)
    even_x, odd_x = swaps(32)
    even_y, odd_y = swaps(8)

    hbm = pl.BlockSpec(memory_space=pltpu.HBM)
    flat = shape(64, 128)
    fields, drag, cell, radius, vel, pos, spin = call(
        deposit_kernel,
        (
            shape(4, 2, 8, 128),
            shape(3, 64, 128),
            shape(64, 128, dtype=jnp.int32),
            flat,
            shape(3, 8192),
            shape(3, 8192),
            shape(3, 8192),
        ),
        [hbm] * 6,
        scratch=[
            pltpu.VMEM((48, 128), F32),
            pltpu.VMEM((8, 64, 128), F32),
            pltpu.SemaphoreType.DMA((6,)),
        ],
    )(*in_hbm(cell, fluid, radius, vel, pos, spin))
    table, border = call(
        table_kernel,
        (shape(320, 512, dtype=BF16), shape(10, 16, 128)),
        [VMEM_SPEC] * 5,
    )(pos, vel, spin, radius, cell)

    even_side = lax.ppermute(fields, "gy", even_y)
    odd_side = lax.ppermute(fields, "gy", odd_y)
    near, slim = call(
        rows_kernel,
        (shape(96, 128), shape(4, 2, 8, 128)),
        [VMEM_SPEC] * 3,
    )(fields, even_side, odd_side)
    near, slim, border = lax.optimization_barrier((near, slim, border))
    near_b = lax.ppermute(near, "gx", odd_x)
    far_b = lax.ppermute(slim, "gx", [(i, ((i + 2) ^ 2) - 2) for i in range(2, 30)])
    near_a = lax.ppermute(near, "gx", even_x)
    far_a = lax.ppermute(slim, "gx", [(i, i ^ 2) for i in range(32)])
    ghost = lax.ppermute(border, "gx", [(i, i + 1) for i in range(31)])
    sums, basis = call(
        krylov_kernel, (shape(256, 128), shape(3, 2, 8, 128)), [VMEM_SPEC] * 5, cost=work(8),
    )(near, near_b, near_a, far_b, far_a)
    every = lax.all_to_all(sums, BOTH, 0, 0, tiled=True)

    table, sums = lax.optimization_barrier((table, sums))
    sums_384 = pltpu.VMEM((384, 256), F32)
    found = pltpu.VMEM((10, BLOCKS, 128), F32)
    twelve = shape(12, BLOCKS, 128)
    parts_p, parts_q, back, before = call(
        contact_kernel,
        (twelve, twelve, shape(6, 16, 128), shape(6, 64, 128)),
        [SMEM_SPEC] + [VMEM_SPEC] * 3,
        scratch=[
            found,
            found,
            pltpu.VMEM((400, 512), BF16),
            pltpu.VMEM((192, 256), F32),
            sums_384,
            sums_384,
        ],
        cost=work(2),
    )(live, pairs, table, ghost)
    returned = lax.ppermute(back, "gx", [(i + 1, i) for i in range(31)])
    total = call(
        own_kernel,
        shape(6, 64, 128),
        [SMEM_SPEC] + [VMEM_SPEC] * 4,
        scratch=[sums_384, sums_384],
        cost=work(1),
    )(live, pairs, parts_p, parts_q, before)
    return call(
        finish_kernel,
        (shape(3, 8192), shape(3, 8192), shape(2, 8, 128)),
        [VMEM_SPEC] * 5,
    )(total, returned, drag, every, basis)


def solution(mesh):
    return jax.shard_map(
        per_device,
        mesh=mesh,
        in_specs=(
            P(None, BOTH),
            P(None, BOTH),
            P(None, BOTH),
            P(BOTH),
            P(BOTH),
            P(BOTH, None, None),
            P(BOTH),
            P(None, "gx", "gy", None),
        ),
        out_specs=(P(None, BOTH), P(None, BOTH), P("gx", "gy", None)),
        check_vma=False,
    )
```

```python
import functools

import jax
import jax.numpy as jnp
from jax import lax
from jax.experimental import pallas as pl
from jax.experimental.pallas import tpu as pltpu
from jax.sharding import PartitionSpec as P

STIFFNESS = 4.0
DAMPING = 1.0
FRICTION = 0.5
SLIP_SCALE = 0.1
DRAG_RATE = 3.0
SPHERE = 4.18879020478639

F32 = jnp.float32
BF16 = jnp.bfloat16
BOTH = ("gx", "gy")
VMEM_SPEC = pl.BlockSpec(memory_space=pltpu.VMEM)
SMEM_SPEC = pl.BlockSpec(memory_space=pltpu.SMEM)
PARAMS = pltpu.CompilerParams(vmem_limit_bytes=24 * 1024 * 1024)


def split(x):
    high = x.astype(BF16)
    return high, (x - high.astype(F32)).astype(BF16)


def one_hot(size, index):
    rows = lax.broadcasted_iota(jnp.int32, (size, index.shape[1]), 0)
    return rows == index


def hot_rows(size, index):
    rows = lax.broadcasted_iota(jnp.int32, (size, 128), 0).astype(F32).astype(BF16)
    out = []
    for k in range(index.shape[1] // 128):
        here = index[:, 128 * k : 128 * k + 128].astype(F32)
        here = jnp.broadcast_to(here, (size, 128)).astype(BF16)
        out.append(jnp.where(rows == here, jnp.ones((), BF16), jnp.zeros((), BF16)))
    return jnp.concatenate(out, axis=1)


def as_bf16(mask):
    return jnp.where(mask, 1.0, 0.0).astype(BF16)


def lanes(block, rows):
    return jnp.concatenate([block[r : r + 1, :] for r in rows], axis=1)


def dot_nt(left, right):
    return lax.dot_general(left, right, (((1,), (1,)), ((), ())), preferred_element_type=F32)


def fold(blocks):
    sub = lax.broadcasted_iota(jnp.int32, (8, 128), 0)
    for step in (4, 2, 1):
        low = (sub & step) == 0
        half = len(blocks) // 2
        blocks = [
            jnp.where(
                low,
                blocks[i] + pltpu.roll(blocks[i], 8 - step, 0),
                blocks[i + half] + pltpu.roll(blocks[i + half], step, 0),
            )
            for i in range(half)
        ]
    return blocks[0]


def tiles(x):
    return [x[:, 128 * k : 128 * k + 128] for k in range(x.shape[1] // 128)]


def halves(x):
    high = x.astype(BF16).astype(F32)
    return high, (x - high).astype(BF16).astype(F32)


def dense(ref, d, count=64):
    return jnp.concatenate(
        [ref[d : d + 1, 128 * k : 128 * k + 128] for k in range(count)], axis=0
    )


def spread(ref, v, row, masks):
    value = jnp.broadcast_to(ref[v, pl.ds(row, 1), :], (16, 128)).astype(BF16)
    return [value * m for m in masks]


def load_all(sources, targets, sems):
    copies = [
        pltpu.make_async_copy(src, dst, sems.at[k])
        for k, (src, dst) in enumerate(zip(sources, targets))
    ]
    for copy in copies:
        copy.start()
    return copies


def deposit_kernel(
    cell_in, fluid_in, radius_in, vel_in, pos_in, spin_in,
    fields, drag, cell, radius, vel, pos, spin, fluid, parts, sems,
):
    copies = load_all(
        (cell_in, fluid_in, radius_in, vel_in, pos_in, spin_in),
        (cell, fluid, radius, vel, pos, spin),
        sems,
    )
    for copy in copies[:2]:
        copy.wait()
    fluid_high, fluid_low = split(fluid[...])
    fluid_table = jnp.concatenate([fluid_high, fluid_low], axis=1)
    total = jnp.zeros((128, 128), F32)
    for g in range(8):
        rows = slice(8 * g, 8 * g + 8)
        cells = lanes(cell[rows, :], range(8))
        hot = hot_rows(128, cells & 127)
        mask = one_hot(16, cells >> 7)
        seen = jnp.dot(
            fluid_table, jnp.concatenate([hot, hot], axis=0), preferred_element_type=F32
        )
        if g == 0:
            for copy in copies[2:4]:
                copy.wait()
        rad = radius[rows, :]
        values = []
        for d in range(3):
            chosen = jnp.where(mask, seen[16 * d : 16 * d + 16], 0.0)
            u = fold(tiles(chosen[0:8] + chosen[8:16]))
            v = jnp.concatenate(
                [vel[d : d + 1, 1024 * g + 128 * k : 1024 * g + 128 * k + 128] for k in range(8)],
                axis=0,
            )
            force = DRAG_RATE * rad * (u - v)
            drag[d, rows, :] = force
            values.append(-force)
        values.append(SPHERE * rad * rad * rad)
        for k, value in enumerate(values):
            high, low = halves(value)
            parts[k, rows, :] = high
            parts[4 + k, rows, :] = low
        masks = tiles(hot_rows(16, cells >> 7))
        left = [
            jnp.concatenate([spread(parts, v, 8 * g + k, masks[k : k + 1])[0] for v in range(8)], 0)
            for k in range(8)
        ]
        total = total + dot_nt(jnp.concatenate(left, axis=1), hot)
    total = total[0:64] + total[64:128]
    lane = lax.broadcasted_iota(jnp.int32, (16, 128), 1)
    mz = total[32:48]
    up = jnp.where(lane == 127, 0.0, pltpu.roll(mz, 127, 1))
    down = jnp.where(lane == 0, 0.0, pltpu.roll(mz, 1, 1))
    out = [total[0:16], 1.0 / (1.0 + total[48:64]), total[16:32], 0.5 * (up - down)]
    for f in range(4):
        for layer in range(2):
            fields[f, layer] = out[f][8 * layer : 8 * layer + 8]
    for copy in copies[4:]:
        copy.wait()


def table_kernel(pos, vel, spin, radius, cell, table, border):
    place = (lax.axis_index("gx"), lax.axis_index("gy"))
    cells = cell[...]
    rad = radius[...]
    corner = [
        place[0] * 2 + (cells >> 10),
        place[1] * 8 + ((cells >> 7) & 7),
        cells & 127,
    ]
    fields = [dense(pos, d) - corner[d].astype(F32) for d in range(3)]
    fields += [dense(vel, d) for d in range(3)]
    fields += [rad * dense(spin, d) for d in range(3)]
    fields += [rad]
    for f in range(10):
        high, low = split(fields[f])
        rows = pl.ds(32 * f, 32)
        table[rows, 0:128] = high[0:32]
        table[rows, 128:256] = high[32:64]
        table[rows, 256:384] = low[0:32]
        table[rows, 384:512] = low[32:64]
        border[f] = fields[f][0:16] - 1.0 if f == 0 else fields[f][0:16]


BLOCKS = 32


def first_index(block):
    index = lanes(block, range(0, 16, 2))
    return (index >> 7) & 31, (index & 127) + ((index >> 12) << 7)


def second_index(block):
    index = lanes(block, range(1, 16, 2))
    beyond = index - 8192
    row = jnp.where(beyond >= 0, 32 + ((beyond >> 7) & 7), (index >> 7) & 31)
    side = jnp.where(beyond >= 0, beyond >> 10, index >> 12)
    return row, (index & 127) + (side << 7)


def groups(live):
    return (jnp.minimum(live, BLOCKS) + 7) // 8


def pair_block(pairs, it):
    return pairs[pl.ds(pl.multiple_of(it * 16, 16), 16), :]


def gather(table, row, place, beyond):
    out = [[] for _ in range(10)]
    for part in range(2):
        here = slice(512 * part, 512 * part + 512)
        hot = hot_rows(256, place[:, here])
        mask = one_hot(32, row[:, here])
        seen = jnp.dot(table[...], jnp.concatenate([hot, hot], axis=0), preferred_element_type=F32)
        for f in range(10):
            s = jnp.where(mask, seen[32 * f : 32 * f + 32], 0.0)
            s = (s[0:8] + s[8:16]) + (s[16:24] + s[24:32])
            if beyond:
                mask_far = one_hot(8, row[:, here] - 32)
                s = s + jnp.where(mask_far, seen[320 + 8 * f : 328 + 8 * f], 0.0)
            out[f] += tiles(s)
    return [fold(x) for x in out]


def cross(a, b):
    return [
        a[1] * b[2] - a[2] * b[1],
        a[2] * b[0] - a[0] * b[2],
        a[0] * b[1] - a[1] * b[0],
    ]


def dot3(a, b):
    return a[0] * b[0] + a[1] * b[1] + a[2] * b[2]


def contact_terms(first, second):
    offset = [second[d] - first[d] for d in range(3)]
    distance = jnp.sqrt(dot3(offset, offset))
    reach = first[9] + second[9]
    inverse = 1.0 / jnp.maximum(distance, 0.25 * reach)
    normal = [o * inverse for o in offset]
    correlation = jnp.maximum(reach - distance, 0.0)
    root = jnp.sqrt(correlation)
    lever = [first[6 + d] + second[6 + d] for d in range(3)]
    turn = cross(lever, normal)
    slip = [second[3 + d] - first[3 + d] - turn[d] for d in range(3)]
    speed = dot3(slip, normal)
    push = STIFFNESS * correlation * root - DAMPING * root * speed
    tangent = [slip[d] - speed * normal[d] for d in range(3)]
    size = jnp.sqrt(dot3(tangent, tangent) + SLIP_SCALE * SLIP_SCALE)
    scale = FRICTION * jnp.abs(push) / size
    friction = [scale * t for t in tangent]
    force = [friction[d] - push * normal[d] for d in range(3)]
    twist = cross(normal, friction)
    return force, twist


def contact_kernel(
    live, pairs, table, ghost,
    parts_p, parts_q, back, total, first, second, full, sum_far, sum_p, sum_q,
):
    count = live[0]
    full[0:320, :] = table[...]
    pieces = [
        jnp.concatenate([ghost[f, 0:8, :], ghost[f, 8:16, :]], axis=1) for f in range(10)
    ]
    high, low = split(jnp.concatenate(pieces, axis=0))
    full[320:400, 0:256] = high
    full[320:400, 256:512] = low

    def look(it, carry):
        block = pair_block(pairs, it)
        rows = pl.ds(pl.multiple_of(it * 8, 8), 8)
        p = gather(table, *first_index(block), False)
        q = gather(full, *second_index(block), True)
        for f in range(10):
            first[f, rows, :] = p[f]
            second[f, rows, :] = q[f]
        return carry

    lax.fori_loop(0, groups(count), look, 0)
    p = [first[f] for f in range(10)]
    q = [second[f] for f in range(10)]
    force, twist = contact_terms(p, q)
    keep = lax.broadcasted_iota(jnp.int32, (BLOCKS, 128), 0) < count
    to_p = force + [p[9] * v for v in twist]
    to_q = [-v for v in force] + [q[9] * v for v in twist]
    for k in range(6):
        for parts, values in ((parts_p, to_p), (parts_q, to_q)):
            high, low = halves(jnp.where(keep, values[k], 0.0))
            parts[k] = high
            parts[6 + k] = low
    sum_far[...] = jnp.zeros_like(sum_far)

    def step(it, carry):
        row, place = second_index(pair_block(pairs, it))
        hot = hot_rows(256, place)
        far = hot_rows(16, row - 32)
        left = [
            jnp.concatenate(
                sum([spread(parts_q, v, it * 8 + k, [m]) for v in range(12)], []), axis=0
            )
            for k, m in enumerate(tiles(far))
        ]
        sum_far[...] += dot_nt(jnp.concatenate(left, axis=1), hot)
        return carry

    lax.fori_loop(0, groups(count), step, 0)
    for f in range(6):
        rows = sum_far[16 * f : 16 * f + 8, :] + sum_far[96 + 16 * f : 104 + 16 * f, :]
        back[f, 0:8, :] = rows[:, 0:128]
        back[f, 8:16, :] = rows[:, 128:256]

    @pl.when(early())
    def _():
        own_sums(live, pairs, parts_p, parts_q, total, sum_p, sum_q)


def early():
    gx = lax.axis_index("gx")
    return (gx > 0) & ((gx & 7) == 0)


def own_sums(live, pairs, parts_p, parts_q, total, sum_p, sum_q):
    sum_p[...] = jnp.zeros_like(sum_p)
    sum_q[...] = jnp.zeros_like(sum_q)

    def step(it, carry):
        block = pair_block(pairs, it)
        for index, parts, sums in (
            (first_index, parts_p, sum_p),
            (second_index, parts_q, sum_q),
        ):
            row, place = index(block)
            hot = hot_rows(256, place)
            mask = hot_rows(32, row)
            left = [
                jnp.concatenate(
                    sum([spread(parts, v, it * 8 + k, [m[0:16], m[16:32]]) for v in range(12)], []),
                    axis=0,
                )
                for k, m in enumerate(tiles(mask))
            ]
            sums[...] += dot_nt(jnp.concatenate(left, axis=1), hot)
        return carry

    lax.fori_loop(0, groups(live[0]), step, 0)
    for f in range(6):
        rows = slice(32 * f, 32 * f + 32)
        rest = slice(192 + 32 * f, 224 + 32 * f)
        own = (sum_p[rows, :] + sum_p[rest, :]) + (sum_q[rows, :] + sum_q[rest, :])
        total[f, 0:32, :] = own[:, 0:128]
        total[f, 32:64, :] = own[:, 128:256]


def own_kernel(live, pairs, parts_p, parts_q, before, total, sum_p, sum_q):
    @pl.when(early())
    def _():
        total[...] = before[...]

    @pl.when(jnp.logical_not(early()))
    def _():
        own_sums(live, pairs, parts_p, parts_q, total, sum_p, sum_q)


def finish_kernel(total, returned, drag, sums, basis, force_out, twist_out, pressure):
    solve(sums, basis, pressure)
    for f in range(3):
        for g in range(8):
            rows = slice(8 * g, 8 * g + 8)
            force = total[f, rows, :] + drag[f, rows, :]
            twist = total[3 + f, rows, :]
            if g < 2:
                force = force + returned[f, rows, :]
                twist = twist + returned[3 + f, rows, :]
            for k in range(8):
                at = slice(1024 * g + 128 * k, 1024 * g + 128 * k + 128)
                force_out[f : f + 1, at] = force[k : k + 1]
                twist_out[f : f + 1, at] = twist[k : k + 1]


def next_row(x):
    return pltpu.roll(x, x.shape[0] - 1, 0)


def last_row(x):
    return pltpu.roll(x, 1, 0)


def rows_kernel(own, even_side, odd_side, near, slim):
    even = (lax.axis_index("gy") & 1) == 0
    sub = lax.broadcasted_iota(jnp.int32, (8, 128), 0)

    def extend(f, layer):
        e, o = even_side[f, layer], odd_side[f, layer]
        after = jnp.where(even, e, o)
        before = jnp.where(even, o, e)
        return jnp.concatenate([own[f, layer], jnp.where(sub < 4, after, before)], axis=0)

    def put(f, layer, x):
        near[32 * f + 16 * layer : 32 * f + 16 * layer + 16, :] = x

    for layer in range(2):
        mx = extend(0, layer)
        my = extend(2, layer)
        part = extend(3, layer) + 0.5 * (next_row(my) - last_row(my))
        put(0, layer, mx)
        put(1, layer, extend(1, layer))
        put(2, layer, part)
        slim[0, layer] = mx[0:8]
        slim[1, layer] = mx[8:16]
        slim[2, layer] = own[1, layer]
        slim[3, layer] = part[0:8]


SHIFT = 3.0


def krylov_kernel(own, near_b, near_a, far_b, far_a, sums, basis):
    gx, gy = lax.axis_index("gx"), lax.axis_index("gy")
    up_a = (gx & 1) == 0
    far_up_a = (gx & 2) == 0
    blank = jnp.zeros((8, 128), F32)

    def layers(f):
        def far(ref, s):
            if f == 0:
                return jnp.concatenate([ref[0, s], ref[1, s]], axis=0)
            return jnp.concatenate([ref[1 + f, s], blank], axis=0)

        pick = lambda cond, u, v: [jnp.where(cond, x, y) for x, y in zip(u, v)]
        near = lambda ref, s: ref[32 * f + 16 * s : 32 * f + 16 * s + 16, :]
        a = [near(near_a, s) for s in range(2)]
        b = [near(near_b, s) for s in range(2)]
        c = [far(far_a, s) for s in range(2)]
        d = [far(far_b, s) for s in range(2)]
        return (
            pick(far_up_a, d, c)
            + pick(up_a, b, a)
            + [near(own, 0), near(own, 1)]
            + pick(up_a, a, b)
            + pick(far_up_a, c, d)
        )

    mx, por, part = layers(0), layers(1), layers(2)
    row = lax.broadcasted_iota(jnp.int32, (16, 128), 0)
    lane = lax.broadcasted_iota(jnp.int32, (16, 128), 1)
    inside_y = (row < 8) | ((row < 12) & (gy < 7)) | ((row >= 12) & (gy > 0))

    def inside(l):
        x = gx * 2 + (l - 4)
        return inside_y & (x >= 0) & (x < 64)

    masks = [inside(l) for l in range(10)]
    zplus = lambda x: jnp.where(lane == 127, 0.0, pltpu.roll(x, 127, 1))
    zminus = lambda x: jnp.where(lane == 0, 0.0, pltpu.roll(x, 1, 1))
    half = [0.5 * p for p in por]
    wx = [half[l] + half[l + 1] for l in range(9)]
    wy = [h + next_row(h) for h in half]
    wy_low = [last_row(w) for w in wy]
    wz = [h + zplus(h) for h in half]
    wz_low = [h + zminus(h) for h in half]

    def apply(p, l):
        c = p[l]
        return (
            wx[l] * (c - p[l + 1])
            + wx[l - 1] * (c - p[l - 1])
            + wy[l] * (c - next_row(c))
            + wy_low[l] * (c - last_row(c))
            + wz[l] * (c - zplus(c))
            + wz_low[l] * (c - zminus(c))
        )

    v0 = {
        l: jnp.where(masks[l], part[l] + 0.5 * (mx[l + 1] - mx[l - 1]), 0.0) for l in range(1, 9)
    }
    a0 = {l: apply(v0, l) for l in range(2, 8)}
    v1 = {l: jnp.where(masks[l], a0[l] * (1.0 / SHIFT) - v0[l], 0.0) for l in a0}
    a1 = {l: apply(v1, l) for l in range(3, 7)}
    v2 = {l: jnp.where(masks[l], a1[l] * (1.0 / SHIFT) - v1[l], 0.0) for l in a1}
    a2 = {l: apply(v2, l) for l in range(4, 6)}

    def inner(p, q):
        return p[4][0:8] * q[4][0:8] + p[5][0:8] * q[5][0:8]

    products = [
        inner(v0, a0),
        inner(v1, a0),
        inner(v2, a0),
        inner(v1, a1),
        inner(v2, a1),
        inner(v2, a2),
        inner(v0, v0),
        inner(v1, v0),
    ]
    at = lax.broadcasted_iota(jnp.int32, (8, 128), 1)
    sub = lax.broadcasted_iota(jnp.int32, (8, 128), 0)
    eight = jnp.sum(fold(products), axis=1, keepdims=True)
    ninth = jnp.sum(inner(v2, v0), keepdims=True)
    line = jnp.sum(jnp.where(at == sub, eight, 0.0), axis=0, keepdims=True)
    line = line + jnp.where(at[0:1] == 8, ninth, 0.0)
    sums[...] = jnp.broadcast_to(line, (256, 128))
    for s in range(2):
        basis[0, s] = v0[4 + s][0:8]
        basis[1, s] = v1[4 + s][0:8]
        basis[2, s] = v2[4 + s][0:8]


def solve(sums, basis, pressure):
    line = jnp.sum(sums[...], axis=0, keepdims=True)
    at = lax.broadcasted_iota(jnp.int32, (1, 128), 1)
    h00, h01, h02, h11, h12, h22, g0, g1, g2 = [
        jnp.sum(jnp.where(at == k, line, 0.0), axis=1, keepdims=True) for k in range(9)
    ]
    l10 = h01 / h00
    l20 = h02 / h00
    d1 = h11 - l10 * h01
    e = h12 - l10 * h02
    l21 = e / d1
    d2 = h22 - l20 * h02 - l21 * e
    y1 = g1 - l10 * g0
    y2 = g2 - l20 * g0 - l21 * y1
    c2 = y2 / d2
    c1 = y1 / d1 - l21 * c2
    c0 = g0 / h00 - l10 * c1 - l20 * c2
    for s in range(2):
        pressure[s] = c0 * basis[0, s] + c1 * basis[1, s] + c2 * basis[2, s]


def shape(*dims, dtype=F32):
    return jax.ShapeDtypeStruct(dims, dtype)


def call(kernel, out, specs, outs=None, scratch=(), cost=None, **more):
    return pl.pallas_call(
        kernel,
        out_shape=out,
        in_specs=specs,
        out_specs=outs if outs is not None else jax.tree.map(lambda _: VMEM_SPEC, out),
        scratch_shapes=scratch,
        compiler_params=PARAMS,
        cost_estimate=cost,
        **more,
    )


def work(us):
    return pl.CostEstimate(flops=us * 10**9, bytes_accessed=0, transcendentals=0)


def in_hbm(*arrays):
    return [pltpu.with_memory_space_constraint(x, pltpu.HBM) for x in arrays]


def swaps(count):
    even = [(i, i ^ 1) for i in range(count)]
    odd = [(i, ((i + 1) ^ 1) - 1) for i in range(1, count - 1)]
    return even, odd


def per_device(pos, vel, spin, radius, cell, pairs, live, fluid):
    radius = radius.reshape(64, 128)
    cell = cell.reshape(64, 128)
    pairs = pairs.reshape(128, 128)
    fluid = fluid.reshape(48, 128)
    even_x, odd_x = swaps(32)
    even_y, odd_y = swaps(8)

    hbm = pl.BlockSpec(memory_space=pltpu.HBM)
    flat = shape(64, 128)
    fields, drag, cell, radius, vel, pos, spin = call(
        deposit_kernel,
        (
            shape(4, 2, 8, 128),
            shape(3, 64, 128),
            shape(64, 128, dtype=jnp.int32),
            flat,
            shape(3, 8192),
            shape(3, 8192),
            shape(3, 8192),
        ),
        [hbm] * 6,
        scratch=[
            pltpu.VMEM((48, 128), F32),
            pltpu.VMEM((8, 64, 128), F32),
            pltpu.SemaphoreType.DMA((6,)),
        ],
    )(*in_hbm(cell, fluid, radius, vel, pos, spin))
    table, border = call(
        table_kernel,
        (shape(320, 512, dtype=BF16), shape(10, 16, 128)),
        [VMEM_SPEC] * 5,
    )(pos, vel, spin, radius, cell)

    even_side = lax.ppermute(fields, "gy", even_y)
    odd_side = lax.ppermute(fields, "gy", odd_y)
    near, slim = call(
        rows_kernel,
        (shape(96, 128), shape(4, 2, 8, 128)),
        [VMEM_SPEC] * 3,
    )(fields, even_side, odd_side)
    near, slim, border = lax.optimization_barrier((near, slim, border))
    near_b = lax.ppermute(near, "gx", odd_x)
    far_b = lax.ppermute(slim, "gx", [(i, ((i + 2) ^ 2) - 2) for i in range(2, 30)])
    near_a = lax.ppermute(near, "gx", even_x)
    far_a = lax.ppermute(slim, "gx", [(i, i ^ 2) for i in range(32)])
    ghost = lax.ppermute(border, "gx", [(i, i + 1) for i in range(31)])
    sums, basis = call(
        krylov_kernel, (shape(256, 128), shape(3, 2, 8, 128)), [VMEM_SPEC] * 5, cost=work(8),
    )(near, near_b, near_a, far_b, far_a)
    every = lax.all_to_all(sums, BOTH, 0, 0, tiled=True)

    table, sums = lax.optimization_barrier((table, sums))
    sums_384 = pltpu.VMEM((384, 256), F32)
    found = pltpu.VMEM((10, BLOCKS, 128), F32)
    twelve = shape(12, BLOCKS, 128)
    parts_p, parts_q, back, before = call(
        contact_kernel,
        (twelve, twelve, shape(6, 16, 128), shape(6, 64, 128)),
        [SMEM_SPEC] + [VMEM_SPEC] * 3,
        scratch=[
            found,
            found,
            pltpu.VMEM((400, 512), BF16),
            pltpu.VMEM((192, 256), F32),
            sums_384,
            sums_384,
        ],
        cost=work(2),
    )(live, pairs, table, ghost)
    returned = lax.ppermute(back, "gx", [(i + 1, i) for i in range(31)])
    total = call(
        own_kernel,
        shape(6, 64, 128),
        [SMEM_SPEC] + [VMEM_SPEC] * 4,
        scratch=[sums_384, sums_384],
        cost=work(1),
    )(live, pairs, parts_p, parts_q, before)
    return call(
        finish_kernel,
        (shape(3, 8192), shape(3, 8192), shape(2, 8, 128)),
        [VMEM_SPEC] * 5,
    )(total, returned, drag, every, basis)


def solution(mesh):
    return jax.shard_map(
        per_device,
        mesh=mesh,
        in_specs=(
            P(None, BOTH),
            P(None, BOTH),
            P(None, BOTH),
            P(BOTH),
            P(BOTH),
            P(BOTH, None, None),
            P(BOTH),
            P(None, "gx", "gy", None),
        ),
        out_specs=(P(None, BOTH), P(None, BOTH), P("gx", "gy", None)),
        check_vma=False,
    )
```
